256 devices in a mesh: wide: 64 (over x, z, y_lo), narrow: 4 (over y_hi, core).
Axes of the slice: x: 4, y: 4 (y_hi: 2, y_lo: 2; y = y_hi * 2 + y_lo), z: 8, core: 2. Of those that a mesh axis runs over, the one named last changes fastest.
Arguments:
- queries: bfloat16 [32768, 8192], P(('wide', 'narrow')), may hold values from -10 to 10
- keys: bfloat16 [32768, 512], P(('wide', 'narrow')), may hold values from -10 to 10
- values: bfloat16 [32768, 512], P(('wide', 'narrow')), may hold values from -6 to 6
- block_order: int32 [64, 2], replicated, may hold values from 0 to 127, as said below
- doc_lengths: int32 [64], replicated, may hold values from 1 to 768, 32768 in all
Outputs:
- attended: float32 [32768, 8192], P(('wide', 'narrow'))
The draws below stay inside these ranges and needn't reach their ends.
Inputs may be any that keep to these rules, and one draw needn't show every extreme that they name: `block_order`: row w holds the two blocks w and 2 * 64 - 1 - w, in either order.
All inputs are finite; a program needn't handle non-finite values.
Results may differ from the reference program's by a relative error of at most 0.002.
Values may be sent and summed in bfloat16 or wider, within the bound.
A program may use at most 128 MiB of HBM per device.

```python
import math
import jax
import jax.numpy as jnp
import numpy as np
from jax import lax

TOK_DEV = 128
QUERY_HEADS = 64
KV_HEADS = 4
HEAD_DIM = 128
REACH = 3
GROUP = 256
SEQ = 32768
DOC_MOST = 768
NDOCS = 64
N_WIDE = 64
N_NARROW = 4


def draw_keys(key, part):
    key = jax.random.fold_in(key, 3)
    base_draw = jax.random.truncated_normal(key, -10.0, 10.0, (SEQ, KV_HEADS * HEAD_DIM), jnp.float32)
    return base_draw.astype(jnp.bfloat16)


def draw_queries(key, part):
    key = jax.random.fold_in(key, 5)
    base_draw = jax.random.truncated_normal(key, -10.0, 10.0, (SEQ, QUERY_HEADS * HEAD_DIM), jnp.float32)
    return base_draw.astype(jnp.bfloat16)


def draw_block_order(key, part):
    key = jax.random.fold_in(key, 7)
    wide_count = SEQ // (2 * GROUP)
    flipped = jax.random.randint(key, (wide_count,), 0, 2)
    first_ids = jnp.arange(wide_count, dtype=jnp.int32)
    second_ids = 2 * wide_count - 1 - first_ids
    left_ids = jnp.where(flipped == 1, second_ids, first_ids)
    right_ids = jnp.where(flipped == 1, first_ids, second_ids)
    return jnp.stack([left_ids, right_ids], axis=1).astype(jnp.int32)


def block_levels(stream_key, extent, shards, low, top_value):
    loudness = 1.0
    for axis_at, parts in shards:
        heights = jax.random.uniform(jax.random.fold_in(jax.random.fold_in(stream_key, 6), axis_at), (parts,), jnp.float32, low / len(shards), top_value / len(shards))
        loudness = loudness * jnp.repeat(jnp.exp(heights), extent[axis_at] // parts).reshape((-1,) + (1,) * (len(extent) - 1 - axis_at))
    return loudness


def length_profile(count, total, most, skew):
    weights = [(1 << 20) // math.isqrt(standing ** skew) + 1 for standing in range(2, count + 1)]
    rest, counts = total - most - (count - 1), [1] * (count - 1)
    while rest > 0:
        free = [i for i in range(count - 1) if counts[i] < most]
        pool, budget = sum([weights[i] for i in free]), rest
        for i in free:
            extra = min(most - counts[i], max(1, budget * weights[i] // pool), rest)
            counts[i] = counts[i] + extra
            rest = rest - extra
    return np.array([most] + counts)


def uneven_parts(key, count, total, bound, slope):
    if count == 2:
        one = jax.random.randint(key, (), max(1, total - bound), min(bound, total - 1) + 1)
        return jnp.stack([one, total - one])
    tallies = jnp.asarray(length_profile(count, total, bound, slope), jnp.int32)
    twos = (count - 1) // 2
    donor, receiver = tallies[1:1 + 2 * twos:2], tallies[2:2 + 2 * twos:2]
    room = jnp.minimum(donor - 1, bound - receiver)
    passed = jax.random.randint(jax.random.fold_in(key, 1), (twos,), 0, 1 << 20) % (room + 1)
    tallies = tallies.at[1:1 + 2 * twos:2].set(donor - passed).at[2:2 + 2 * twos:2].set(receiver + passed)
    return tallies[jax.random.permutation(jax.random.fold_in(key, 2), count)]


def noise(rng, dims, width, limit, shards=(), kind=jnp.bfloat16):
    values = jax.random.normal(rng, dims, jnp.float32) * width
    if len(shards) > 0:
        values = block_levels(rng, dims, shards, -0.22, 0.18) * values
    return jnp.clip(values, min=-limit, max=limit).astype(kind)


def setup_inputs(seed: int = 0) -> dict:
    key_list = jax.random.split(jax.random.key(seed), 6)
    return {
        "queries": draw_queries(jax.random.fold_in(key_list[5], 71), 0),
        "keys": draw_keys(jax.random.fold_in(key_list[5], 71), 0),
        "values": noise(key_list[2], (SEQ, KV_HEADS * HEAD_DIM), 1.0, 6.0, ((0, 256),)),
        "block_order": draw_block_order(jax.random.fold_in(key_list[5], 71), 0),
        "doc_lengths": uneven_parts(key_list[4], NDOCS, SEQ, DOC_MOST, 2).astype(jnp.int32),
    }


def doc_index(positions, doc_ends):
    return lax.optimization_barrier(jnp.sum((positions[:, None] >= doc_ends[None, :]).astype(jnp.int32), axis=1))

def reference(queries, keys, values, block_order, doc_lengths):
    half_rows = TOK_DEV // 2
    head_share = QUERY_HEADS // KV_HEADS
    starts = block_order.astype(jnp.int32)[:, None, :, None] * GROUP + (jnp.arange(N_NARROW, dtype=jnp.int32) * half_rows)[None, :, None, None] + jnp.arange(half_rows, dtype=jnp.int32)[None, None, None, :]
    positions = starts.reshape(-1).astype(jnp.int32)
    seq_q = jnp.zeros_like(queries).at[positions].set(queries)
    seq_k = jnp.zeros_like(keys).at[positions].set(keys)
    seq_v = jnp.zeros_like(values).at[positions].set(values)
    pad_rows = REACH * GROUP
    padded_k = jnp.concatenate([jnp.zeros((pad_rows, keys.shape[1]), keys.dtype), seq_k], axis=0)
    padded_v = jnp.concatenate([jnp.zeros((pad_rows, values.shape[1]), values.dtype), seq_v], axis=0)
    doc_ends = jnp.cumsum(doc_lengths).astype(jnp.int32)
    score_scale = 1.0 / math.sqrt(HEAD_DIM)
    key_span = (REACH + 1) * GROUP

    def one_block(block_id):
        q_rows = lax.dynamic_slice_in_dim(seq_q, block_id * GROUP, GROUP, 0).astype(jnp.float32)
        q_rows = q_rows.reshape(GROUP, KV_HEADS, head_share, HEAD_DIM)
        k_rows = lax.dynamic_slice_in_dim(padded_k, block_id * GROUP, key_span, 0).astype(jnp.float32)
        k_rows = k_rows.reshape(key_span, KV_HEADS, HEAD_DIM)
        v_rows = lax.dynamic_slice_in_dim(padded_v, block_id * GROUP, key_span, 0).astype(jnp.float32)
        v_rows = v_rows.reshape(key_span, KV_HEADS, HEAD_DIM)
        q_pos = block_id * GROUP + jnp.arange(GROUP, dtype=jnp.int32)
        k_pos = (block_id - REACH) * GROUP + jnp.arange(key_span, dtype=jnp.int32)
        visible = (k_pos[None, :] <= q_pos[:, None]) & (doc_index(k_pos, doc_ends)[None, :] == doc_index(q_pos, doc_ends)[:, None]) & (k_pos[None, :] >= 0)
        scores = jnp.einsum('qhgd,khd->hgqk', q_rows, k_rows) * score_scale
        scores = jnp.where(visible[None, None], scores, -1e+30)
        row_max = lax.optimization_barrier(jnp.max(scores, axis=-1, keepdims=True))
        weights = jnp.exp(scores - row_max)
        weight_sum = lax.optimization_barrier(jnp.sum(weights, axis=-1, keepdims=True))
        rounded = lax.optimization_barrier(weights.astype(jnp.bfloat16)).astype(jnp.float32)
        mixed_out = jnp.einsum('hgqk,khd->hgqd', rounded, v_rows) / weight_sum
        return mixed_out.transpose(2, 0, 1, 3).reshape(GROUP, QUERY_HEADS * HEAD_DIM)
    blocks_out = lax.map(one_block, jnp.arange(2 * N_WIDE, dtype=jnp.int32))
    seq_out = blocks_out.reshape(SEQ, QUERY_HEADS * HEAD_DIM)
    return seq_out[positions]
```

```python
import functools
import math

import jax
import jax.numpy as jnp
from jax import lax
from jax.experimental import pallas as pl
from jax.experimental.pallas import tpu as pltpu
from jax.sharding import PartitionSpec as P

MESH = pl.DeviceIdType.MESH
QUERY_HEADS = 64
KV_HEADS = 4
HEAD_DIM = 128
SHARE = QUERY_HEADS // KV_HEADS
GROUP = 256
ROWS = 64
CHUNKS = 13
KEYS = CHUNKS * ROWS
NDOCS = 64
OWN = 6
FLOW = 7
LAST = 31
MASKED = -1e30


class Place:
    def __init__(self):
        self.w = lax.axis_index("wide")
        self.n = lax.axis_index("narrow")
        self.g = self.w // 2
        self.ylo = self.w % 2
        self.yhi = self.n // 2
        self.c = self.n % 2
        self.across = self.w + 1 - 2 * self.ylo
        self.sibling = self.n + 1 - 2 * self.c


class Exchange:
    def __init__(self, place, win, send_sem, recv_sem, sib_sem):
        self.p = place
        self.win, self.send_sem, self.recv_sem, self.sib_sem = win, send_sem, recv_sem, sib_sem
        self.draining = False

    @staticmethod
    def at(slot):
        return 13 if isinstance(slot, int) and slot == FLOW else 2 * slot

    def chunk(self, s, h, slot):
        return self.win(s, h).at[self.at(slot)]

    def _send(self, cond, s, h, k, src, dst, recv, device):
        def copy():
            return pltpu.make_async_remote_copy(
                src_ref=src, dst_ref=dst, send_sem=self.send_sem.at[s, h, k], recv_sem=recv,
                device_id=device, device_id_type=MESH,
            )

        def go():
            copy().wait_send() if self.draining else copy().start()

        go() if cond is None else pl.when(cond)(go)

    def between(self, s):
        return (self.p.g < LAST, 2) if s == 0 else (self.p.g > 0, -2)

    def put(self, cond, s, h, k, slot, device, to_s, to):
        dst = self.win(to_s, h).at[self.at(to)]
        self._send(cond, s, h, k, self.chunk(s, h, slot), dst, self.recv_sem.at[to_s, h, to], device)

    def onward(self, s, h, slot, cond=None):
        p = self.p
        goes, step = self.between(s)
        goes = goes if cond is None else jnp.logical_and(goes, cond)
        self.put(goes, s, h, 6 - slot, slot, (p.w + step, p.n), s, slot - 4)

    def spread(self, s, h, slot, cond):
        p = self.p
        self.put(cond, s, h, 3, slot, (p.across, p.c), s, 4 + p.yhi)
        self.put(cond, s, h, 4, slot, (p.across, 2 + p.c), s, 3 + p.yhi)

    def fold(self, h):
        p = self.p
        both = jnp.logical_and
        near = both(p.g == LAST - 1, p.ylo == 1)
        here = p.g == LAST
        self.put(near, 0, h, 7, OWN, (p.w + 2, p.n), 1, 0)
        self.put(both(near, p.yhi == 1), 0, h, 8, OWN, (p.w + 2, p.c), 1, 1)
        self.put(here, 0, h, 0, OWN, (p.across, p.n), 1, 2)
        self.put(both(here, p.yhi == 0), 0, h, 1, OWN, (p.across, p.n + 2), 1, 1)
        self.put(both(both(here, p.ylo == 0), p.yhi == 1), 0, h, 1, OWN, (p.w, p.n - 2), 1, 1)
        self.inside(both(here, p.ylo == 0), h, 1, 0)
        for slot in range(3):
            self.inside(p.g == 0, h, 0, slot)

    def share(self, s, h, slot, cond=None):
        if self.draining:
            return
        p = self.p
        if slot == 0:
            cond = p.c == 1 if cond is None else jnp.logical_and(cond, p.c == 1)
        if slot == OWN:
            cond = p.c == 0 if cond is None else jnp.logical_and(cond, p.c == 0)
        at = slot - 1 + p.c
        src, dst = self.chunk(s, h, slot), self.win(s, h).at[2 * at + 1]

        def go():
            pltpu.make_async_remote_copy(
                src_ref=src, dst_ref=dst, send_sem=self.sib_sem.at[0, s, h], recv_sem=self.sib_sem.at[1, s, h],
                device_id=(p.w, p.sibling), device_id_type=MESH,
            ).start()

        go() if cond is None else pl.when(cond)(go)

    def inside(self, cond, h, s, slot):
        if self.draining:
            return
        pl.when(cond)(
            lambda: pltpu.make_async_copy(
                self.chunk(0, h, OWN), self.chunk(s, h, slot), self.recv_sem.at[s, h, slot]
            ).start()
        )

    def await_slot(self, s, h, slot, cond=None):
        if self.draining:
            return
        if cond is not None:
            pl.when(cond)(lambda: self.await_slot(s, h, slot))
            return
        ref = self.chunk(s, h, slot)
        pltpu.make_async_copy(ref, ref, self.recv_sem.at[s, h, slot]).wait()

    def roles(self, s):
        p = self.p
        first = p.ylo == s
        second = p.ylo != s
        low, high = p.yhi == 0, p.yhi == 1
        both = jnp.logical_and
        return first, second, both(first, low), both(first, high), both(second, low), both(second, high)

    def over(self, s, h, k, slot, half, to, cond):
        self.put(cond, s, h, k, slot, (self.p.across, 2 * half + self.p.c), s, to)

    def phase(self, number, s, h):
        p = self.p
        F, S, Fl, Fh, Sl, Sh = self.roles(s)
        low, high = p.yhi == 0, p.yhi == 1
        parity = h % 2
        carrier = jnp.logical_and(F, p.yhi == parity)

        def take(slot, cond=None, on=False):
            self.await_slot(s, h, slot, cond)
            if on:
                self.onward(s, h, slot, cond)

        if number == 0:
            self.onward(s, h, OWN)
            self.spread(s, h, OWN, F)
            self.over(s, h, 5, OWN, parity, FLOW, Sl)
            self.share(s, h, OWN)
            if s == 0:
                self.fold(h)
        elif number == 1:
            take(2)
            self.spread(s, h, 2, S)
            self.share(s, h, 2)
            take(5, Sl, True)
            self.share(s, h, 5, Sl)
            take(4, S, True)
            self.share(s, h, 4, S)
            take(3, Sh)
            self.over(s, h, 5, 3, 1, 5, Sh)
            self.share(s, h, 3, Sh)
            take(FLOW, carrier)
            self.over(s, h, 6, FLOW, 1, 5, carrier)
        elif number == 2:
            take(0, S)
            self.over(s, h, 6, 0, 0, 3, Sh)
            self.share(s, h, 0, S)
            take(1, Sl)
            self.share(s, h, 1, Sl)
            take(5, Fl)
            self.over(s, h, 5, 5, 0, 3, Fl)
            self.onward(s, h, 5, Fl)
            self.share(s, h, 5, Fl)
            take(4, F, True)
            self.share(s, h, 4, F)
            take(3, Fh)
            self.share(s, h, 3, Fh)
            take(5, high, True)
            self.share(s, h, 5, high)
        elif number == 3:
            take(3, low)
            self.share(s, h, 3, low)
            take(0, F)
            self.share(s, h, 0, F)
            rest = jnp.logical_not(Sl)
            take(1, rest)
            self.share(s, h, 1, rest)

    def arrived(self, s, h):
        ref = self.win(s, h).at[0:6]
        for way in (1, 0):
            pltpu.make_async_copy(ref, ref, self.sib_sem.at[way, s, h]).wait()


def greet(p):
    barrier = pltpu.get_barrier_semaphore()

    def signal(device):
        pl.semaphore_signal(barrier, inc=1, device_id=device, device_id_type=MESH)

    def pair(wide):
        signal((wide, p.c))
        signal((wide, 2 + p.c))

    both = jnp.logical_and
    top = p.g // LAST
    below = p.g // (LAST - 1) - top
    up, down = 1 - top, 1 - (LAST - p.g) // LAST
    pair(p.across)
    signal((p.w, p.sibling))
    pl.when(p.g < LAST)(lambda: signal((p.w + 2, p.n)))
    pl.when(p.g > 0)(lambda: signal((p.w - 2, p.n)))
    pl.when(both(p.g == LAST, p.ylo == 0))(lambda: signal((p.w, p.n + 2 - 4 * p.yhi)))
    pl.when(both(both(p.g == LAST - 1, p.ylo == 1), p.yhi == 1))(lambda: signal((p.w + 2, p.c)))
    pl.when(both(both(p.g == LAST, p.ylo == 1), p.yhi == 0))(lambda: signal((p.w - 2, 2 + p.c)))
    turn = p.ylo * (below * p.yhi + top * (1 - p.yhi)) + top * (1 - p.ylo)
    pl.semaphore_wait(barrier, 3 + up + down + turn)


def masks(start, lengths_ref, key_side, query_side):
    lane = lax.broadcasted_iota(jnp.int32, (1, 128), 1)
    begins = jnp.zeros((1, 128), jnp.int32)
    ends = jnp.zeros((1, 128), jnp.int32)
    for e in range(NDOCS):
        length = lengths_ref[e]
        begins = begins + jnp.where(lane > e, length, 0)
        ends = ends + jnp.where(lane >= e, length, 0)
    lanes = lax.broadcasted_iota(jnp.int32, (KEYS, 128), 1)
    place = lax.broadcasted_iota(jnp.int32, (KEYS, 128), 0) - (KEYS - ROWS)
    pos = place + start
    in_doc = ((pos >= begins) & (pos < ends)) | (pos < 0)
    own = place == lanes - NDOCS
    key_side[...] = jnp.where(((lanes < NDOCS) & in_doc) | ((lanes >= NDOCS) & own), 1.0, 0.0).astype(jnp.bfloat16)
    lanes = lax.broadcasted_iota(jnp.int32, (ROWS, 128), 1)
    row = lax.broadcasted_iota(jnp.int32, (ROWS, 128), 0)
    pos = row + start
    other = (pos < begins) | (pos >= ends)
    later = lanes - NDOCS > row
    query_side[...] = jnp.where(((lanes < NDOCS) & other) | (later & (lanes >= NDOCS)), MASKED, 0.0).astype(jnp.bfloat16)


TILE_HEADS = 4
PARTS = ((0, 256), (256, 512), (512, 768), (768, 896))


def attend(q_ref, side_ref, keys_side_ref, win_ref, h, row, write):
    rate = math.log2(math.e) / math.sqrt(HEAD_DIM)
    k = win_ref[:, :, 0:HEAD_DIM].reshape(KEYS, HEAD_DIM)
    v = win_ref[:, :, HEAD_DIM : 2 * HEAD_DIM].reshape(KEYS, HEAD_DIM)
    k = jnp.concatenate([k, keys_side_ref[...]], axis=1)
    v = jnp.concatenate([v, jnp.ones((KEYS, HEAD_DIM), jnp.bfloat16)], axis=1)
    k = jnp.concatenate([k, k[KEYS - ROWS :]], axis=0)
    v = jnp.concatenate([v, jnp.zeros((ROWS, 2 * HEAD_DIM), jnp.bfloat16)], axis=0)
    side = side_ref[...]
    tiles = SHARE // TILE_HEADS

    def columns(a):
        return pl.ds(pl.multiple_of((h * SHARE + a) * HEAD_DIM, HEAD_DIM), HEAD_DIM)

    def queries(t):
        heads = range(t * TILE_HEADS, (t + 1) * TILE_HEADS)
        return jnp.concatenate(
            [jnp.concatenate([q_ref[row : row + ROWS, columns(a)], side], axis=1) for a in heads], axis=0
        )

    def score(q, part):
        low, high = part
        return lax.dot_general(q, k[low:high], (((1,), (1,)), ((), ())), preferred_element_type=jnp.float32)

    q = queries(0)
    ahead = [score(q, part) for part in PARTS]
    for t in range(tiles):
        scores, ahead = ahead, []
        if t + 1 < tiles:
            q = queries(t + 1)
        top = functools.reduce(
            jnp.maximum, [s[:, at : at + 128] for s in scores for at in range(0, s.shape[1], 128)]
        )
        top = jnp.max(top, axis=1, keepdims=True)
        mixed = None
        for part, s in zip(PARTS, scores):
            if t + 1 < tiles:
                ahead.append(score(q, part))
            weights = jnp.exp2((s - top) * rate).astype(jnp.bfloat16)
            new = jnp.dot(weights, v[part[0] : part[1]], preferred_element_type=jnp.float32)
            mixed = new if mixed is None else mixed + new
        mixed = mixed[:, 0:HEAD_DIM] / mixed[:, HEAD_DIM : 2 * HEAD_DIM]
        for i in range(TILE_HEADS):
            write(columns(t * TILE_HEADS + i), mixed[i * ROWS : (i + 1) * ROWS])


def kernel(
    order_hbm, lengths_hbm, q_hbm, k_hbm, v_hbm, out_ref, order_ref, lengths_ref, q_ref, k_ref, v_ref, win, key_side,
    query_side, in_sem, send_sem, recv_sem, sib_sem,
):
    p = Place()
    loads = [
        pltpu.make_async_copy(src, dst, in_sem.at[i])
        for i, (src, dst) in enumerate(
            ((order_hbm, order_ref), (k_hbm, k_ref), (v_hbm, v_ref), (lengths_hbm, lengths_ref), (q_hbm, q_ref))
        )
    ]
    for load in loads:
        load.start()
    greet(p)
    for load in loads[:4]:
        load.wait()
    first = order_ref[0, p.w]

    def swapped(width):
        return jnp.full((ROWS, width), first, jnp.int32) >= 64

    def own(h):
        cols = pl.ds(pl.multiple_of(h * HEAD_DIM, HEAD_DIM), HEAD_DIM)
        other = swapped(HEAD_DIM)
        for part, ref in enumerate((k_ref, v_ref)):
            low, high = ref[0:ROWS, cols], ref[ROWS : 2 * ROWS, cols]
            to = slice(part * HEAD_DIM, (part + 1) * HEAD_DIM)
            win[0, h, 12, :, to] = jnp.where(other, high, low)
            win[1, h, 12, :, to] = jnp.where(other, low, high)
        for s in range(2):
            ex.phase(0, s, h)

    ex = Exchange(p, lambda s, h: win.at[s, h], send_sem, recv_sem, sib_sem)

    def turn_queries(i, carry):
        wide = 1024
        cols = pl.ds(pl.multiple_of(i * wide, wide), wide)
        low, high = q_ref[0:ROWS, cols], q_ref[ROWS : 2 * ROWS, cols]
        other = swapped(wide)
        q_ref[0:ROWS, cols] = jnp.where(other, high, low)
        q_ref[ROWS : 2 * ROWS, cols] = jnp.where(other, low, high)
        return carry

    def late_rows(cols, mixed):
        out_ref[ROWS : 2 * ROWS, cols] = mixed

    def early_rows(cols, mixed):
        late = out_ref[ROWS : 2 * ROWS, cols]
        other = swapped(HEAD_DIM)
        out_ref[0:ROWS, cols] = jnp.where(other, late, mixed)
        out_ref[ROWS : 2 * ROWS, cols] = jnp.where(other, mixed, late)

    def unit(s, h):
        ex.arrived(s, h)
        write = late_rows if s == 1 else early_rows
        attend(q_ref, query_side.at[s], key_side.at[s], win.at[s, h, 0:CHUNKS], h, s * ROWS, write)

    def both(number, h):
        for s in range(2):
            ex.phase(number, s, h)

    def fill(t, carry):
        own(t)

        @pl.when(t == 0)
        def _():
            masks(p.w * GROUP + p.n * ROWS, lengths_ref, key_side.at[0], query_side.at[0])
            masks((2 * 64 - 1 - p.w) * GROUP + p.n * ROWS, lengths_ref, key_side.at[1], query_side.at[1])

        @pl.when(t == 1)
        def _():
            loads[4].wait()
            lax.fori_loop(0, 8, turn_queries, 0)

        for number in range(1, 4):
            pl.when(t >= number)(lambda number=number: both(number, t - number))
        return carry

    def work(h, carry):
        pl.when(h + 3 < KV_HEADS)(lambda: both(1, h + 3))
        unit(1, h)
        for number, later in ((2, 2), (3, 1)):
            pl.when(h + later < KV_HEADS)(lambda number=number, later=later: both(number, h + later))
        unit(0, h)
        return carry

    lax.fori_loop(0, KV_HEADS, fill, 0)
    lax.fori_loop(0, KV_HEADS, work, 0)
    ex.draining = True

    def drain(h, carry):
        for number in range(3):
            both(number, h)
        return carry

    lax.fori_loop(0, KV_HEADS, drain, 0)


def attention(block_order, doc_lengths, queries, keys, values):
    held = pl.BlockSpec(memory_space=pltpu.HBM)
    flops = 2 * 2 * ROWS * QUERY_HEADS * KEYS * 512
    operands = [
        pltpu.with_memory_space_constraint(a, pltpu.HBM) for a in (block_order, doc_lengths, queries, keys, values)
    ]
    return pl.pallas_call(
        kernel,
        out_shape=pltpu.VMEM(queries.shape, jnp.float32),
        in_specs=[held] * 5,
        out_specs=pl.BlockSpec(memory_space=pltpu.VMEM),
        scratch_shapes=[
            pltpu.SMEM((2, 64), jnp.int32),
            pltpu.SMEM((NDOCS,), jnp.int32),
            pltpu.VMEM((2 * ROWS, QUERY_HEADS * HEAD_DIM), jnp.bfloat16),
            pltpu.VMEM((2 * ROWS, KV_HEADS * HEAD_DIM), jnp.bfloat16),
            pltpu.VMEM((2 * ROWS, KV_HEADS * HEAD_DIM), jnp.bfloat16),
            pltpu.VMEM((2, KV_HEADS, CHUNKS + 1, ROWS, 2 * HEAD_DIM), jnp.bfloat16),
            pltpu.VMEM((2, KEYS, HEAD_DIM), jnp.bfloat16),
            pltpu.VMEM((2, ROWS, HEAD_DIM), jnp.bfloat16),
            pltpu.SemaphoreType.DMA((5,)),
            pltpu.SemaphoreType.DMA((2, KV_HEADS, 9)),
            pltpu.SemaphoreType.DMA((2, KV_HEADS, 8)),
            pltpu.SemaphoreType.DMA((2, 2, KV_HEADS)),
        ],
        compiler_params=pltpu.CompilerParams(collective_id=0, has_side_effects=True, vmem_limit_bytes=40 << 20),
        cost_estimate=pl.CostEstimate(flops=flops, bytes_accessed=10 << 20, transcendentals=0),
        name="exchange_attend",
    )(*operands)


def body(queries, keys, values, block_order, doc_lengths):
    return attention(block_order.T, doc_lengths, queries, keys, values)


def solution(mesh):
    rows = P(("wide", "narrow"), None)
    return jax.shard_map(
        body, mesh=mesh, in_specs=(rows, rows, rows, P(), P()), out_specs=rows, check_vma=False
    )
```

```python
import functools
import math

import jax
import jax.numpy as jnp
from jax import lax
from jax.experimental import pallas as pl
from jax.experimental.pallas import tpu as pltpu
from jax.sharding import PartitionSpec as P

MESH = pl.DeviceIdType.MESH
QUERY_HEADS = 64
KV_HEADS = 4
HEAD_DIM = 128
SHARE = QUERY_HEADS // KV_HEADS
GROUP = 256
ROWS = 64
CHUNKS = 13
KEYS = CHUNKS * ROWS
NDOCS = 64
OWN = 6
FLOW = 7
LAST = 31
MASKED = -1e30


class Place:
    def __init__(self):
        self.w = lax.axis_index("wide")
        self.n = lax.axis_index("narrow")
        self.g = self.w // 2
        self.ylo = self.w % 2
        self.yhi = self.n // 2
        self.c = self.n % 2
        self.across = self.w + 1 - 2 * self.ylo
        self.sibling = self.n + 1 - 2 * self.c


class Exchange:
    def __init__(self, place, win, send_sem, recv_sem, sib_sem):
        self.p = place
        self.win, self.send_sem, self.recv_sem, self.sib_sem = win, send_sem, recv_sem, sib_sem
        self.draining = False

    @staticmethod
    def at(slot):
        return 13 if isinstance(slot, int) and slot == FLOW else 2 * slot

    def chunk(self, s, h, slot):
        return self.win(s, h).at[self.at(slot)]

    def _send(self, cond, s, h, k, src, dst, recv, device):
        def copy():
            return pltpu.make_async_remote_copy(
                src_ref=src, dst_ref=dst, send_sem=self.send_sem.at[s, h, k], recv_sem=recv,
                device_id=device, device_id_type=MESH,
            )

        def go():
            copy().wait_send() if self.draining else copy().start()

        go() if cond is None else pl.when(cond)(go)

    def between(self, s):
        return (self.p.g < LAST, 2) if s == 0 else (self.p.g > 0, -2)

    def put(self, cond, s, h, k, slot, device, to_s, to):
        dst = self.win(to_s, h).at[self.at(to)]
        self._send(cond, s, h, k, self.chunk(s, h, slot), dst, self.recv_sem.at[to_s, h, to], device)

    def onward(self, s, h, slot, cond=None):
        p = self.p
        goes, step = self.between(s)
        goes = goes if cond is None else jnp.logical_and(goes, cond)
        self.put(goes, s, h, 6 - slot, slot, (p.w + step, p.n), s, slot - 4)

    def spread(self, s, h, slot, cond):
        p = self.p
        self.put(cond, s, h, 3, slot, (p.across, p.c), s, 4 + p.yhi)
        self.put(cond, s, h, 4, slot, (p.across, 2 + p.c), s, 3 + p.yhi)

    def fold(self, h):
        p = self.p
        both = jnp.logical_and
        near = both(p.g == LAST - 1, p.ylo == 1)
        here = p.g == LAST
        self.put(near, 0, h, 7, OWN, (p.w + 2, p.n), 1, 0)
        self.put(both(near, p.yhi == 1), 0, h, 8, OWN, (p.w + 2, p.c), 1, 1)
        self.put(here, 0, h, 0, OWN, (p.across, p.n), 1, 2)
        self.put(both(here, p.yhi == 0), 0, h, 1, OWN, (p.across, p.n + 2), 1, 1)
        self.put(both(both(here, p.ylo == 0), p.yhi == 1), 0, h, 1, OWN, (p.w, p.n - 2), 1, 1)
        self.inside(both(here, p.ylo == 0), h, 1, 0)
        for slot in range(3):
            self.inside(p.g == 0, h, 0, slot)

    def share(self, s, h, slot, cond=None):
        if self.draining:
            return
        p = self.p
        if slot == 0:
            cond = p.c == 1 if cond is None else jnp.logical_and(cond, p.c == 1)
        if slot == OWN:
            cond = p.c == 0 if cond is None else jnp.logical_and(cond, p.c == 0)
        at = slot - 1 + p.c
        src, dst = self.chunk(s, h, slot), self.win(s, h).at[2 * at + 1]

        def go():
            pltpu.make_async_remote_copy(
                src_ref=src, dst_ref=dst, send_sem=self.sib_sem.at[0, s, h], recv_sem=self.sib_sem.at[1, s, h],
                device_id=(p.w, p.sibling), device_id_type=MESH,
            ).start()

        go() if cond is None else pl.when(cond)(go)

    def inside(self, cond, h, s, slot):
        if self.draining:
            return
        pl.when(cond)(
            lambda: pltpu.make_async_copy(
                self.chunk(0, h, OWN), self.chunk(s, h, slot), self.recv_sem.at[s, h, slot]
            ).start()
        )

    def await_slot(self, s, h, slot, cond=None):
        if self.draining:
            return
        if cond is not None:
            pl.when(cond)(lambda: self.await_slot(s, h, slot))
            return
        ref = self.chunk(s, h, slot)
        pltpu.make_async_copy(ref, ref, self.recv_sem.at[s, h, slot]).wait()

    def roles(self, s):
        p = self.p
        first = p.ylo == s
        second = p.ylo != s
        low, high = p.yhi == 0, p.yhi == 1
        both = jnp.logical_and
        return first, second, both(first, low), both(first, high), both(second, low), both(second, high)

    def over(self, s, h, k, slot, half, to, cond):
        self.put(cond, s, h, k, slot, (self.p.across, 2 * half + self.p.c), s, to)

    def phase(self, number, s, h):
        p = self.p
        F, S, Fl, Fh, Sl, Sh = self.roles(s)
        low, high = p.yhi == 0, p.yhi == 1
        parity = h % 2
        carrier = jnp.logical_and(F, p.yhi == parity)

        def take(slot, cond=None, on=False):
            self.await_slot(s, h, slot, cond)
            if on:
                self.onward(s, h, slot, cond)

        if number == 0:
            self.onward(s, h, OWN)
            self.spread(s, h, OWN, F)
            self.over(s, h, 5, OWN, parity, FLOW, Sl)
            self.share(s, h, OWN)
            if s == 0:
                self.fold(h)
        elif number == 1:
            take(2)
            self.spread(s, h, 2, S)
            self.share(s, h, 2)
            take(5, Sl, True)
            self.share(s, h, 5, Sl)
            take(4, S, True)
            self.share(s, h, 4, S)
            take(3, Sh)
            self.over(s, h, 5, 3, 1, 5, Sh)
            self.share(s, h, 3, Sh)
            take(FLOW, carrier)
            self.over(s, h, 6, FLOW, 1, 5, carrier)
        elif number == 2:
            take(0, S)
            self.over(s, h, 6, 0, 0, 3, Sh)
            self.share(s, h, 0, S)
            take(1, Sl)
            self.share(s, h, 1, Sl)
            take(5, Fl)
            self.over(s, h, 5, 5, 0, 3, Fl)
            self.onward(s, h, 5, Fl)
            self.share(s, h, 5, Fl)
            take(4, F, True)
            self.share(s, h, 4, F)
            take(3, Fh)
            self.share(s, h, 3, Fh)
            take(5, high, True)
            self.share(s, h, 5, high)
        elif number == 3:
            take(3, low)
            self.share(s, h, 3, low)
            take(0, F)
            self.share(s, h, 0, F)
            rest = jnp.logical_not(Sl)
            take(1, rest)
            self.share(s, h, 1, rest)

    def arrived(self, s, h):
        ref = self.win(s, h).at[0:6]
        for way in (1, 0):
            pltpu.make_async_copy(ref, ref, self.sib_sem.at[way, s, h]).wait()


def greet(p):
    barrier = pltpu.get_barrier_semaphore()

    def signal(device):
        pl.semaphore_signal(barrier, inc=1, device_id=device, device_id_type=MESH)

    def pair(wide):
        signal((wide, p.c))
        signal((wide, 2 + p.c))

    both = jnp.logical_and
    top = p.g // LAST
    below = p.g // (LAST - 1) - top
    up, down = 1 - top, 1 - (LAST - p.g) // LAST
    pair(p.across)
    signal((p.w, p.sibling))
    pl.when(p.g < LAST)(lambda: signal((p.w + 2, p.n)))
    pl.when(p.g > 0)(lambda: signal((p.w - 2, p.n)))
    pl.when(both(p.g == LAST, p.ylo == 0))(lambda: signal((p.w, p.n + 2 - 4 * p.yhi)))
    pl.when(both(both(p.g == LAST - 1, p.ylo == 1), p.yhi == 1))(lambda: signal((p.w + 2, p.c)))
    pl.when(both(both(p.g == LAST, p.ylo == 1), p.yhi == 0))(lambda: signal((p.w - 2, 2 + p.c)))
    turn = p.ylo * (below * p.yhi + top * (1 - p.yhi)) + top * (1 - p.ylo)
    pl.semaphore_wait(barrier, 3 + up + down + turn)


def masks(start, lengths_ref, key_side, query_side):
    lane = lax.broadcasted_iota(jnp.int32, (1, 128), 1)
    begins = jnp.zeros((1, 128), jnp.int32)
    ends = jnp.zeros((1, 128), jnp.int32)
    for e in range(NDOCS):
        length = lengths_ref[e]
        begins = begins + jnp.where(lane > e, length, 0)
        ends = ends + jnp.where(lane >= e, length, 0)
    lanes = lax.broadcasted_iota(jnp.int32, (KEYS, 128), 1)
    place = lax.broadcasted_iota(jnp.int32, (KEYS, 128), 0) - (KEYS - ROWS)
    pos = place + start
    in_doc = ((pos >= begins) & (pos < ends)) | (pos < 0)
    own = place == lanes - NDOCS
    key_side[...] = jnp.where(((lanes < NDOCS) & in_doc) | ((lanes >= NDOCS) & own), 1.0, 0.0).astype(jnp.bfloat16)
    lanes = lax.broadcasted_iota(jnp.int32, (ROWS, 128), 1)
    row = lax.broadcasted_iota(jnp.int32, (ROWS, 128), 0)
    pos = row + start
    other = (pos < begins) | (pos >= ends)
    later = lanes - NDOCS > row
    query_side[...] = jnp.where(((lanes < NDOCS) & other) | (later & (lanes >= NDOCS)), MASKED, 0.0).astype(jnp.bfloat16)


TILE_HEADS = 4
PARTS = ((0, 256), (256, 512), (512, 768), (768, 896))


def attend(q_ref, side_ref, keys_side_ref, win_ref, h, row, write):
    rate = math.log2(math.e) / math.sqrt(HEAD_DIM)
    k = win_ref[:, :, 0:HEAD_DIM].reshape(KEYS, HEAD_DIM)
    v = win_ref[:, :, HEAD_DIM : 2 * HEAD_DIM].reshape(KEYS, HEAD_DIM)
    k = jnp.concatenate([k, keys_side_ref[...]], axis=1)
    v = jnp.concatenate([v, jnp.ones((KEYS, HEAD_DIM), jnp.bfloat16)], axis=1)
    k = jnp.concatenate([k, k[KEYS - ROWS :]], axis=0)
    v = jnp.concatenate([v, jnp.zeros((ROWS, 2 * HEAD_DIM), jnp.bfloat16)], axis=0)
    side = side_ref[...]
    tiles = SHARE // TILE_HEADS

    def columns(a):
        return pl.ds(pl.multiple_of((h * SHARE + a) * HEAD_DIM, HEAD_DIM), HEAD_DIM)

    def queries(t):
        heads = range(t * TILE_HEADS, (t + 1) * TILE_HEADS)
        return jnp.concatenate(
            [jnp.concatenate([q_ref[row : row + ROWS, columns(a)], side], axis=1) for a in heads], axis=0
        )

    def score(q, part):
        low, high = part
        return lax.dot_general(q, k[low:high], (((1,), (1,)), ((), ())), preferred_element_type=jnp.float32)

    q = queries(0)
    ahead = [score(q, part) for part in PARTS]
    for t in range(tiles):
        scores, ahead = ahead, []
        if t + 1 < tiles:
            q = queries(t + 1)
        top = functools.reduce(
            jnp.maximum, [s[:, at : at + 128] for s in scores for at in range(0, s.shape[1], 128)]
        )
        top = jnp.max(top, axis=1, keepdims=True)
        mixed = None
        for part, s in zip(PARTS, scores):
            if t + 1 < tiles:
                ahead.append(score(q, part))
            weights = jnp.exp2((s - top) * rate).astype(jnp.bfloat16)
            new = jnp.dot(weights, v[part[0] : part[1]], preferred_element_type=jnp.float32)
            mixed = new if mixed is None else mixed + new
        mixed = mixed[:, 0:HEAD_DIM] / mixed[:, HEAD_DIM : 2 * HEAD_DIM]
        for i in range(TILE_HEADS):
            write(t * TILE_HEADS + i, mixed[i * ROWS : (i + 1) * ROWS])


def kernel(
    order_hbm, lengths_hbm, q_hbm, k_hbm, v_hbm, out_ref, win, q_ref, key_side, query_side, order_ref, lengths_ref, k_ref,
    v_ref, in_sem, send_sem, recv_sem, sib_sem,
):
    p = Place()
    loads = [
        pltpu.make_async_copy(src, dst, in_sem.at[i])
        for i, (src, dst) in enumerate(
            ((order_hbm, order_ref), (k_hbm, k_ref), (v_hbm, v_ref), (lengths_hbm, lengths_ref), (q_hbm, q_ref))
        )
    ]
    for load in loads:
        load.start()
    greet(p)
    for load in loads[:4]:
        load.wait()
    first = order_ref[0, p.w]

    def swapped(width):
        return jnp.full((ROWS, width), first, jnp.int32) >= 64

    def own(h):
        cols = pl.ds(pl.multiple_of(h * HEAD_DIM, HEAD_DIM), HEAD_DIM)
        other = swapped(HEAD_DIM)
        for part, ref in enumerate((k_ref, v_ref)):
            low, high = ref[0:ROWS, cols], ref[ROWS : 2 * ROWS, cols]
            to = slice(part * HEAD_DIM, (part + 1) * HEAD_DIM)
            win[0, h, 12, :, to] = jnp.where(other, high, low)
            win[1, h, 12, :, to] = jnp.where(other, low, high)
        for s in range(2):
            ex.phase(0, s, h)

    ex = Exchange(p, lambda s, h: win.at[s, h], send_sem, recv_sem, sib_sem)

    def turn_queries(i, carry):
        wide = 1024
        cols = pl.ds(pl.multiple_of(i * wide, wide), wide)
        low, high = q_ref[0:ROWS, cols], q_ref[ROWS : 2 * ROWS, cols]
        other = swapped(wide)
        q_ref[0:ROWS, cols] = jnp.where(other, high, low)
        q_ref[ROWS : 2 * ROWS, cols] = jnp.where(other, low, high)
        return carry

    def unit(s, h):
        def write(a, mixed):
            cols = pl.ds(pl.multiple_of((h * SHARE + a) * HEAD_DIM, HEAD_DIM), HEAD_DIM)
            out_ref[s, :, cols] = mixed

        ex.arrived(s, h)
        attend(q_ref, query_side.at[s], key_side.at[s], win.at[s, h, 0:CHUNKS], h, s * ROWS, write)

    def both(number, h):
        for s in range(2):
            ex.phase(number, s, h)

    def fill(t, carry):
        own(t)

        @pl.when(t == 0)
        def _():
            masks(p.w * GROUP + p.n * ROWS, lengths_ref, key_side.at[0], query_side.at[0])
            masks((2 * 64 - 1 - p.w) * GROUP + p.n * ROWS, lengths_ref, key_side.at[1], query_side.at[1])

        @pl.when(t == 1)
        def _():
            loads[4].wait()
            lax.fori_loop(0, 8, turn_queries, 0)

        for number in range(1, 4):
            pl.when(t >= number)(lambda number=number: both(number, t - number))
        return carry

    def work(h, carry):
        pl.when(h + 3 < KV_HEADS)(lambda: both(1, h + 3))
        unit(1, h)
        for number, later in ((2, 2), (3, 1)):
            pl.when(h + later < KV_HEADS)(lambda number=number, later=later: both(number, h + later))
        unit(0, h)
        return carry

    lax.fori_loop(0, KV_HEADS, fill, 0)
    lax.fori_loop(0, KV_HEADS - 1, work, 0)
    for s in range(2):
        ex.arrived(s, KV_HEADS - 1)
    ex.draining = True

    def drain(h, carry):
        for number in range(3):
            both(number, h)
        return carry

    lax.fori_loop(0, KV_HEADS, drain, 0)


def last_kernel(order_hbm, part_ref, win, q_ref, key_side, query_side, out_hbm, order_ref, o_ref, in_sem, out_sem):
    load = pltpu.make_async_copy(order_hbm, order_ref, in_sem)
    load.start()
    width = SHARE * HEAD_DIM
    done = (KV_HEADS - 1) * width
    w = lax.axis_index("wide")

    def unit(s):
        def write(a, mixed):
            o_ref[s, :, a * HEAD_DIM : (a + 1) * HEAD_DIM] = mixed

        attend(
            q_ref, query_side.at[s], key_side.at[s], win.at[s, KV_HEADS - 1, 0:CHUNKS], KV_HEADS - 1, s * ROWS, write
        )

    unit(1)
    load.wait()
    flip = (order_ref[0, w] >= 64).astype(jnp.int32)
    rows = [pl.ds(pl.multiple_of(at * ROWS, ROWS), ROWS) for at in (flip, 1 - flip)]
    copies = [
        pltpu.make_async_copy(part_ref.at[s], out_hbm.at[rows[s], 0:done], out_sem.at[s]) for s in range(2)
    ] + [pltpu.make_async_copy(o_ref.at[s], out_hbm.at[rows[s], done : done + width], out_sem.at[2 + s]) for s in range(2)]
    for i in (3, 1, 0):
        copies[i].start()
    unit(0)
    copies[2].start()
    for copy in copies:
        copy.wait()


def attention(block_order, doc_lengths, queries, keys, values):
    held = pl.BlockSpec(memory_space=pltpu.HBM)
    near = pl.BlockSpec(memory_space=pltpu.VMEM)
    width = SHARE * HEAD_DIM
    flops = 2 * ROWS * SHARE * KEYS * 512
    operands = [
        pltpu.with_memory_space_constraint(a, pltpu.HBM) for a in (block_order, doc_lengths, queries, keys, values)
    ]
    parts = pl.pallas_call(
        kernel,
        out_shape=(
            pltpu.VMEM((2, ROWS, (KV_HEADS - 1) * width), jnp.float32),
            pltpu.VMEM((2, KV_HEADS, CHUNKS + 1, ROWS, 2 * HEAD_DIM), jnp.bfloat16),
            pltpu.VMEM(queries.shape, jnp.bfloat16),
            pltpu.VMEM((2, KEYS, HEAD_DIM), jnp.bfloat16),
            pltpu.VMEM((2, ROWS, HEAD_DIM), jnp.bfloat16),
        ),
        in_specs=[held] * 5,
        out_specs=(near,) * 5,
        scratch_shapes=[
            pltpu.SMEM((2, 64), jnp.int32),
            pltpu.SMEM((NDOCS,), jnp.int32),
            pltpu.VMEM((2 * ROWS, KV_HEADS * HEAD_DIM), jnp.bfloat16),
            pltpu.VMEM((2 * ROWS, KV_HEADS * HEAD_DIM), jnp.bfloat16),
            pltpu.SemaphoreType.DMA((5,)),
            pltpu.SemaphoreType.DMA((2, KV_HEADS, 9)),
            pltpu.SemaphoreType.DMA((2, KV_HEADS, 8)),
            pltpu.SemaphoreType.DMA((2, 2, KV_HEADS)),
        ],
        compiler_params=pltpu.CompilerParams(collective_id=0, has_side_effects=True, vmem_limit_bytes=32 << 20),
        cost_estimate=pl.CostEstimate(flops=6 * flops, bytes_accessed=4 << 20, transcendentals=0),
        name="exchange_attend",
    )(*operands)
    return pl.pallas_call(
        last_kernel,
        out_shape=jax.ShapeDtypeStruct(queries.shape, jnp.float32),
        in_specs=[held] + [near] * 5,
        out_specs=held,
        scratch_shapes=[
            pltpu.SMEM((2, 64), jnp.int32),
            pltpu.VMEM((2, ROWS, width), jnp.float32),
            pltpu.SemaphoreType.DMA,
            pltpu.SemaphoreType.DMA((4,)),
        ],
        compiler_params=pltpu.CompilerParams(vmem_limit_bytes=32 << 20),
        cost_estimate=pl.CostEstimate(flops=2 * flops, bytes_accessed=4 << 20, transcendentals=0),
        name="attend_last",
    )(operands[0], *parts)


def body(queries, keys, values, block_order, doc_lengths):
    return attention(block_order.T, doc_lengths, queries, keys, values)


def solution(mesh):
    rows = P(("wide", "narrow"), None)
    return jax.shard_map(
        body, mesh=mesh, in_specs=(rows, rows, rows, P(), P()), out_specs=rows, check_vma=False
    )
```

```python
import functools
import math

import jax
import jax.numpy as jnp
from jax import lax
from jax.experimental import pallas as pl
from jax.experimental.pallas import tpu as pltpu
from jax.sharding import PartitionSpec as P

MESH = pl.DeviceIdType.MESH
QUERY_HEADS = 64
KV_HEADS = 4
HEAD_DIM = 128
SHARE = QUERY_HEADS // KV_HEADS
GROUP = 256
ROWS = 64
CHUNKS = 13
KEYS = CHUNKS * ROWS
NDOCS = 64
FIRST_HEADS = KV_HEADS - 1
OWN = 6
FLOW = 7
LAST = 31
MASKED = -1e30


class Place:
    def __init__(self):
        self.w = lax.axis_index("wide")
        self.n = lax.axis_index("narrow")
        self.g = self.w // 2
        self.ylo = self.w % 2
        self.yhi = self.n // 2
        self.c = self.n % 2
        self.across = self.w + 1 - 2 * self.ylo
        self.sibling = self.n + 1 - 2 * self.c


class Exchange:
    def __init__(self, place, win, send_sem, recv_sem, sib_sem):
        self.p = place
        self.win, self.send_sem, self.recv_sem, self.sib_sem = win, send_sem, recv_sem, sib_sem

    def chunk(self, s, h, slot):
        return self.win(s, h).at[OWN, 1] if isinstance(slot, int) and slot == FLOW else self.win(s, h).at[slot, 0]

    def put(self, s, h, k, slot, device, to_s, to):
        pltpu.make_async_remote_copy(
            src_ref=self.chunk(s, h, slot), dst_ref=self.chunk(to_s, h, to), send_sem=self.send_sem.at[s, h, k],
            recv_sem=self.recv_sem.at[to_s, h, to], device_id=device, device_id_type=MESH,
        ).start()

    def goes(self, s):
        return self.p.g < LAST if s == 0 else self.p.g > 0

    def onward(self, s, h, *slots):
        p = self.p
        step = 2 if s == 0 else -2

        def go():
            for slot in slots:
                self.put(s, h, 0, slot, (p.w + step, p.n), s, slot - 4)

        pl.when(self.goes(s))(go)

    def spread(self, s, h, slot):
        p = self.p
        self.put(s, h, 1, slot, (p.across, p.c), s, 4 + p.yhi)
        self.put(s, h, 1, slot, (p.across, 2 + p.c), s, 3 + p.yhi)

    def over(self, s, h, k, slot, half, to):
        self.put(s, h, k, slot, (self.p.across, 2 * half + self.p.c), s, to)

    def folds(self):
        p = self.p
        both = jnp.logical_and
        near = both(p.g == LAST - 1, p.ylo == 1)
        here = p.g == LAST
        return (
            (near, 4, (p.w + 2, p.n), 0),
            (both(near, p.yhi == 1), 5, (p.w + 2, p.c), 1),
            (here, 6, (p.across, p.n), 2),
            (both(here, p.yhi == 0), 7, (p.across, p.n + 2), 1),
            (both(both(here, p.ylo == 0), p.yhi == 1), 8, (p.w, p.n - 2), 1),
        )

    def inside(self, h, s, slot):
        pltpu.make_async_copy(
            self.chunk(0, h, OWN), self.chunk(s, h, slot), self.recv_sem.at[s, h, slot]
        ).start()

    def ends(self, h):
        p = self.p
        for cond, k, device, to in self.folds():
            pl.when(cond)(lambda k=k, device=device, to=to: self.put(0, h, k, OWN, device, 1, to))
        pl.when(jnp.logical_and(p.g == LAST, p.ylo == 0))(lambda: self.inside(h, 1, 0))

        @pl.when(p.g == 0)
        def _():
            for slot in range(3):
                self.inside(h, 0, slot)

    def take(self, s, h, *slots):
        for slot in slots:
            ref = self.chunk(s, h, slot)
            pltpu.make_async_copy(ref, ref, self.recv_sem.at[s, h, slot]).wait()

    def role(self, s):
        p = self.p
        return 2 * (p.ylo if s == 0 else 1 - p.ylo) + p.yhi

    def carries(self, s, h):
        return self.role(s) == h % 2

    def phase(self, number, s, h):
        p = self.p
        role = self.role(s)
        parity = h % 2

        def flow():
            self.take(s, h, FLOW)
            self.over(s, h, 3, FLOW, 1, 5)

        def share(low, high):
            to = low - (1 if high == 7 or low == 1 else 0)
            pltpu.make_async_remote_copy(
                src_ref=self.win(s, h).at[low:high, 0], dst_ref=self.win(s, h).at[to : to + high - low, 1],
                send_sem=self.sib_sem.at[0, s, h], recv_sem=self.sib_sem.at[1, s, h],
                device_id=(p.w, p.sibling), device_id_type=MESH,
            ).start()

        if number == 0:
            self.onward(s, h, OWN)
            pl.when(role < 2)(lambda: self.spread(s, h, OWN))
            pl.when(role == 2)(lambda: self.over(s, h, 2, OWN, parity, FLOW))
            if s == 0:
                pl.when(jnp.logical_or(p.g == 0, p.g >= LAST - 1))(lambda: self.ends(h))
        elif number == 1:
            pl.when(role == parity)(flow)

            @pl.when(role == 2)
            def _():
                self.take(s, h, 5, 4)
                self.onward(s, h, 5, 4)

            @pl.when(role == 3)
            def _():
                self.take(s, h, 4, 3)
                self.onward(s, h, 4)
                self.over(s, h, 2, 3, 1, 5)

        elif number == 2:
            self.take(s, h, 2)
            pl.when(role >= 2)(lambda: self.spread(s, h, 2))

        elif number == 3:

            @pl.when(role == 0)
            def _():
                self.take(s, h, 5)
                self.over(s, h, 2, 5, 0, 3)
                self.take(s, h, 4)
                self.onward(s, h, 5, 4)

            @pl.when(role == 1)
            def _():
                self.take(s, h, 4, 3, 5)
                self.onward(s, h, 4, 5)

            pl.when(role == 2)(lambda: self.take(s, h, 0, 1))

            @pl.when(role == 3)
            def _():
                self.take(s, h, 0)
                self.over(s, h, 3, 0, 0, 3)
                self.take(s, h, 5)
                self.onward(s, h, 5)

            pl.when(p.c == 0)(lambda: share(4, 7))
            pl.when(p.c == 1)(lambda: share(4, 6))

        elif number == 4:
            pl.when(role == 0)(lambda: self.take(s, h, 3, 0, 1))
            pl.when(role == 1)(lambda: self.take(s, h, 0, 1))
            pl.when(role == 2)(lambda: self.take(s, h, 3))
            pl.when(role == 3)(lambda: self.take(s, h, 1))
            pl.when(p.c == 0)(lambda: share(1, 4))
            pl.when(p.c == 1)(lambda: share(0, 4))

    def arrived(self, s, h):
        ref = self.win(s, h).at[0:6, 1]
        for way in (1, 0):
            pltpu.make_async_copy(ref, ref, self.sib_sem.at[way, s, h]).wait()

    def drain(self, h):
        p = self.p
        for s in range(2):
            role = self.role(s)

            def sent(k, count, s=s):
                ref = self.win(s, h).at[0:count, 0]
                pltpu.make_async_copy(ref, ref, self.send_sem.at[s, h, k]).wait()

            pl.when(self.goes(s))(lambda sent=sent: sent(0, 3))
            sent(1, 2)
            pl.when(role != 1)(lambda sent=sent: sent(2, 1))
            pl.when(jnp.logical_or(role == 3, role == h % 2))(lambda sent=sent: sent(3, 1))

            if s == 0:

                @pl.when(p.g >= LAST - 1)
                def _(sent=sent):
                    for cond, k, _, _ in self.folds():
                        pl.when(cond)(lambda k=k: sent(k, 1))


def greet(p):
    barrier = pltpu.get_barrier_semaphore()

    def signal(device):
        pl.semaphore_signal(barrier, inc=1, device_id=device, device_id_type=MESH)

    def pair(wide):
        signal((wide, p.c))
        signal((wide, 2 + p.c))

    both = jnp.logical_and
    top = p.g // LAST
    below = p.g // (LAST - 1) - top
    up, down = 1 - top, 1 - (LAST - p.g) // LAST
    pair(p.across)
    signal((p.w, p.sibling))
    pl.when(p.g < LAST)(lambda: signal((p.w + 2, p.n)))
    pl.when(p.g > 0)(lambda: signal((p.w - 2, p.n)))
    pl.when(both(p.g == LAST, p.ylo == 0))(lambda: signal((p.w, p.n + 2 - 4 * p.yhi)))
    pl.when(both(both(p.g == LAST - 1, p.ylo == 1), p.yhi == 1))(lambda: signal((p.w + 2, p.c)))
    pl.when(both(both(p.g == LAST, p.ylo == 1), p.yhi == 0))(lambda: signal((p.w - 2, 2 + p.c)))
    turn = p.ylo * (below * p.yhi + top * (1 - p.yhi)) + top * (1 - p.ylo)
    pl.semaphore_wait(barrier, 3 + up + down + turn)


def masks(start, lengths_ref, key_side, query_side, reach):
    lane = lax.broadcasted_iota(jnp.int32, (1, 128), 1)
    begins = jnp.zeros((1, 128), jnp.int32)
    ends = jnp.zeros((1, 128), jnp.int32)
    for e in range(NDOCS):
        length = lengths_ref[e]
        begins = begins + jnp.where(lane > e, length, 0)
        ends = ends + jnp.where(lane >= e, length, 0)
    back = jnp.where(begins <= start, begins, 0) - (start - (KEYS - ROWS))
    reach[...] = jnp.broadcast_to(back, (8, 128)).astype(jnp.float32)
    lanes = lax.broadcasted_iota(jnp.int32, (KEYS, 128), 1)
    place = lax.broadcasted_iota(jnp.int32, (KEYS, 128), 0) - (KEYS - ROWS)
    pos = place + start
    in_doc = ((pos >= begins) & (pos < ends)) | (pos < 0)
    own = place == lanes - NDOCS
    key_side[...] = jnp.where(((lanes < NDOCS) & in_doc) | ((lanes >= NDOCS) & own), 1.0, 0.0).astype(jnp.bfloat16)
    lanes = lax.broadcasted_iota(jnp.int32, (ROWS, 128), 1)
    row = lax.broadcasted_iota(jnp.int32, (ROWS, 128), 0)
    pos = row + start
    other = (pos < begins) | (pos >= ends)
    later = lanes - NDOCS > row
    query_side[...] = jnp.where(((lanes < NDOCS) & other) | (later & (lanes >= NDOCS)), MASKED, 0.0).astype(jnp.bfloat16)


TILE_HEADS = 4
PARTS = ((0, 256), (256, 512), (512, 768), (768, 896))


def attend(q_ref, side_ref, keys_side_ref, win_ref, h, row, write, base=0):
    rate = math.log2(math.e) / math.sqrt(HEAD_DIM)
    k, v = [
        jnp.concatenate(
            [win_ref[0:OWN, :, :, cols].reshape(KEYS - ROWS, HEAD_DIM), win_ref[OWN, 0, :, cols]], axis=0
        )
        for cols in (slice(0, HEAD_DIM), slice(HEAD_DIM, 2 * HEAD_DIM))
    ]
    k = jnp.concatenate([k, keys_side_ref[...]], axis=1)
    v = jnp.concatenate([v, jnp.ones((KEYS, HEAD_DIM), jnp.bfloat16)], axis=1)
    if base:
        k, v = k[base:], v[base:]
        parts = [(at, at + 256) for at in range(0, KEYS - base, 256)]
    else:
        k = jnp.concatenate([k, k[KEYS - ROWS :]], axis=0)
        v = jnp.concatenate([v, jnp.zeros((ROWS, 2 * HEAD_DIM), jnp.bfloat16)], axis=0)
        parts = PARTS
    side = side_ref[...]
    tiles = SHARE // TILE_HEADS

    def columns(a):
        return pl.ds(pl.multiple_of((h * SHARE + a) * HEAD_DIM, HEAD_DIM), HEAD_DIM)

    def queries(t):
        heads = range(t * TILE_HEADS, (t + 1) * TILE_HEADS)
        return jnp.concatenate(
            [jnp.concatenate([q_ref[row : row + ROWS, columns(a)], side], axis=1) for a in heads], axis=0
        )

    def score(q, part):
        low, high = part
        return lax.dot_general(q, k[low:high], (((1,), (1,)), ((), ())), preferred_element_type=jnp.float32)

    q = queries(0)
    ahead = [score(q, part) for part in parts]
    for t in range(tiles):
        scores, ahead = ahead, []
        if t + 1 < tiles:
            q = queries(t + 1)
        top = functools.reduce(
            jnp.maximum, [s[:, at : at + 128] for s in scores for at in range(0, s.shape[1], 128)]
        )
        top = jnp.max(top, axis=1, keepdims=True)
        mixed = None
        for part, s in zip(parts, scores):
            if t + 1 < tiles:
                ahead.append(score(q, part))
            weights = jnp.exp2((s - top) * rate).astype(jnp.bfloat16)
            new = jnp.dot(weights, v[part[0] : part[1]], preferred_element_type=jnp.float32)
            mixed = new if mixed is None else mixed + new
        mixed = mixed[:, 0:HEAD_DIM] / mixed[:, HEAD_DIM : 2 * HEAD_DIM]
        for i in range(TILE_HEADS):
            write(t * TILE_HEADS + i, mixed[i * ROWS : (i + 1) * ROWS])


def kernel(
    order_hbm, lengths_hbm, q_hbm, k_hbm, v_hbm, out_ref, win, q_ref, key_side, query_side, reach, order_ref, lengths_ref,
    k_ref, v_ref, in_sem, send_sem, recv_sem, sib_sem,
):
    p = Place()
    loads = [
        pltpu.make_async_copy(src, dst, in_sem.at[i])
        for i, (src, dst) in enumerate(
            ((order_hbm, order_ref), (k_hbm, k_ref), (v_hbm, v_ref), (lengths_hbm, lengths_ref), (q_hbm, q_ref))
        )
    ]
    for load in loads:
        load.start()
    greet(p)
    for load in loads[:4]:
        load.wait()
    first = order_ref[0, p.w]
    reach[2] = jnp.full((8, 128), first, jnp.int32).astype(jnp.float32)

    def swapped(width):
        return jnp.full((ROWS, width), first, jnp.int32) >= 64

    def own(h):
        cols = pl.ds(pl.multiple_of(h * HEAD_DIM, HEAD_DIM), HEAD_DIM)
        other = swapped(HEAD_DIM)
        for part, ref in enumerate((k_ref, v_ref)):
            low, high = ref[0:ROWS, cols], ref[ROWS : 2 * ROWS, cols]
            to = slice(part * HEAD_DIM, (part + 1) * HEAD_DIM)
            win[0, h, OWN, 0, :, to] = jnp.where(other, high, low)
            win[1, h, OWN, 0, :, to] = jnp.where(other, low, high)
        for s in range(2):
            ex.phase(0, s, h)

    ex = Exchange(p, lambda s, h: win.at[s, h], send_sem, recv_sem, sib_sem)

    def turn_queries(i, carry):
        wide = 1024
        cols = pl.ds(pl.multiple_of(i * wide, wide), wide)
        low, high = q_ref[0:ROWS, cols], q_ref[ROWS : 2 * ROWS, cols]
        other = swapped(wide)
        q_ref[0:ROWS, cols] = jnp.where(other, high, low)
        q_ref[ROWS : 2 * ROWS, cols] = jnp.where(other, low, high)
        return carry

    def unit(s, h):
        def write(a, mixed):
            cols = pl.ds(pl.multiple_of((h * SHARE + a) * HEAD_DIM, HEAD_DIM), HEAD_DIM)
            out_ref[s, :, cols] = mixed

        ex.arrived(s, h)
        attend(q_ref, query_side.at[s], key_side.at[s], win.at[s, h], h, s * ROWS, write)

    def at(h, heads, do):
        pl.when(jnp.logical_and(h >= 0, h < heads))(lambda: do(h))

    def step(t, carry):
        def relay(number, s, later):
            at(t - later, KV_HEADS, lambda h: ex.phase(number, s, h))

        at(t, KV_HEADS, own)

        @pl.when(t == 0)
        def _():
            masks(p.w * GROUP + p.n * ROWS, lengths_ref, key_side.at[0], query_side.at[0], reach.at[0])
            masks((2 * 64 - 1 - p.w) * GROUP + p.n * ROWS, lengths_ref, key_side.at[1], query_side.at[1], reach.at[1])

        @pl.when(t == 1)
        def _():
            loads[4].wait()
            lax.fori_loop(0, 8, turn_queries, 0)

        relay(1, 0, 1)
        relay(1, 1, 1)
        relay(2, 1, 1)
        relay(2, 0, 1)
        at(t - KV_HEADS, FIRST_HEADS, lambda h: unit(1, h))
        relay(3, 1, 2)
        relay(3, 0, 2)
        relay(4, 1, 3)
        relay(4, 0, 3)
        at(t - KV_HEADS, FIRST_HEADS, lambda h: unit(0, h))
        at(t - KV_HEADS, KV_HEADS, ex.drain)
        return carry

    lax.fori_loop(0, 2 * KV_HEADS, step, 0)
    for s in range(2):
        ex.arrived(s, FIRST_HEADS)


def last_kernel(part_ref, win, q_ref, key_side, query_side, reach, out_hbm, o_ref, part_sem, out_sem):
    width = SHARE * HEAD_DIM
    flip = (jnp.max(reach[2]) >= 64).astype(jnp.int32)
    rows = [pl.ds(pl.multiple_of(at * ROWS, ROWS), ROWS) for at in (flip, 1 - flip)]
    firsts = [
        pltpu.make_async_copy(part_ref.at[s], out_hbm.at[rows[s], 0 : FIRST_HEADS * width], part_sem.at[s])
        for s in range(2)
    ]
    for copy in firsts:
        copy.start()
    backs = [jnp.max(reach[s]) for s in range(2)]

    tiles, wide = SHARE // TILE_HEADS, TILE_HEADS * HEAD_DIM

    def put(s, tile):
        cols = slice(tile * wide, (tile + 1) * wide)
        to = pl.ds(FIRST_HEADS * width + tile * wide, wide)
        return pltpu.make_async_copy(o_ref.at[s, :, cols], out_hbm.at[rows[s], to], out_sem.at[s, tile])

    for s in (1, 0):

        def write(a, mixed, s=s):
            o_ref[s, :, a * HEAD_DIM : (a + 1) * HEAD_DIM] = mixed
            if a % TILE_HEADS == TILE_HEADS - 1:
                put(s, a // TILE_HEADS).start()

        def take(base, s=s, write=write):
            attend(
                q_ref, query_side.at[s], key_side.at[s], win.at[s, FIRST_HEADS], FIRST_HEADS, s * ROWS, write, base
            )

        back = backs[s]
        pl.when(back >= 320)(lambda take=take: take(320))
        pl.when(jnp.logical_and(back >= 64, back < 320))(lambda take=take: take(64))
        pl.when(back < 64)(lambda take=take: take(0))
    for copy in firsts:
        copy.wait()
    for s in range(2):
        for tile in range(tiles):
            put(s, tile).wait()


def attention(block_order, doc_lengths, queries, keys, values):
    held = pl.BlockSpec(memory_space=pltpu.HBM)
    near = pl.BlockSpec(memory_space=pltpu.VMEM)
    width = SHARE * HEAD_DIM
    flops = 2 * ROWS * SHARE * KEYS * 512
    operands = [
        pltpu.with_memory_space_constraint(a, pltpu.HBM) for a in (block_order, doc_lengths, queries, keys, values)
    ]
    parts = pl.pallas_call(
        kernel,
        out_shape=(
            pltpu.VMEM((2, ROWS, FIRST_HEADS * width), jnp.float32),
            pltpu.VMEM((2, KV_HEADS, OWN + 1, 2, ROWS, 2 * HEAD_DIM), jnp.bfloat16),
            pltpu.VMEM(queries.shape, jnp.bfloat16),
            pltpu.VMEM((2, KEYS, HEAD_DIM), jnp.bfloat16),
            pltpu.VMEM((2, ROWS, HEAD_DIM), jnp.bfloat16),
            pltpu.VMEM((3, 8, 128), jnp.float32),
        ),
        in_specs=[held] * 5,
        out_specs=(near,) * 6,
        scratch_shapes=[
            pltpu.SMEM((2, 64), jnp.int32),
            pltpu.SMEM((NDOCS,), jnp.int32),
            pltpu.VMEM((2 * ROWS, KV_HEADS * HEAD_DIM), jnp.bfloat16),
            pltpu.VMEM((2 * ROWS, KV_HEADS * HEAD_DIM), jnp.bfloat16),
            pltpu.SemaphoreType.DMA((5,)),
            pltpu.SemaphoreType.DMA((2, KV_HEADS, 9)),
            pltpu.SemaphoreType.DMA((2, KV_HEADS, 8)),
            pltpu.SemaphoreType.DMA((2, 2, KV_HEADS)),
        ],
        compiler_params=pltpu.CompilerParams(collective_id=0, has_side_effects=True, vmem_limit_bytes=32 << 20),
        cost_estimate=pl.CostEstimate(flops=2 * FIRST_HEADS * flops, bytes_accessed=4 << 20, transcendentals=0),
        name="exchange_attend",
    )(*operands)
    return pl.pallas_call(
        last_kernel,
        out_shape=jax.ShapeDtypeStruct(queries.shape, jnp.float32),
        in_specs=[near] * 6,
        out_specs=held,
        scratch_shapes=[
            pltpu.VMEM((2, ROWS, width), jnp.float32),
            pltpu.SemaphoreType.DMA((2,)),
            pltpu.SemaphoreType.DMA((2, SHARE // TILE_HEADS)),
        ],
        compiler_params=pltpu.CompilerParams(vmem_limit_bytes=32 << 20),
        cost_estimate=pl.CostEstimate(flops=2 * (KV_HEADS - FIRST_HEADS) * flops, bytes_accessed=4 << 20, transcendentals=0),
        name="attend_last",
    )(*parts)


def body(queries, keys, values, block_order, doc_lengths):
    return attention(block_order.T, doc_lengths, queries, keys, values)


def solution(mesh):
    rows = P(("wide", "narrow"), None)
    return jax.shard_map(
        body, mesh=mesh, in_specs=(rows, rows, rows, P(), P()), out_specs=rows, check_vma=False
    )
```

```python
import functools
import math

import jax
import jax.numpy as jnp
from jax import lax
from jax.experimental import pallas as pl
from jax.experimental.pallas import tpu as pltpu
from jax.sharding import PartitionSpec as P

MESH = pl.DeviceIdType.MESH
QUERY_HEADS = 64
KV_HEADS = 4
HEAD_DIM = 128
SHARE = QUERY_HEADS // KV_HEADS
GROUP = 256
ROWS = 64
CHUNKS = 13
KEYS = CHUNKS * ROWS
NDOCS = 64
FIRST_HEADS = KV_HEADS - 1
OWN = 6
FLOW = 7
LAST = 31
MASKED = -1e30


class Place:
    def __init__(self):
        self.w = lax.axis_index("wide")
        self.n = lax.axis_index("narrow")
        self.g = self.w // 2
        self.ylo = self.w % 2
        self.yhi = self.n // 2
        self.c = self.n % 2
        self.across = self.w + 1 - 2 * self.ylo
        self.sibling = self.n + 1 - 2 * self.c


class Exchange:
    def __init__(self, place, win, send_sem, recv_sem, sib_sem):
        self.p = place
        self.win, self.send_sem, self.recv_sem, self.sib_sem = win, send_sem, recv_sem, sib_sem
        self.draining = False

    @staticmethod
    def at(slot):
        return 13 if isinstance(slot, int) and slot == FLOW else 2 * slot

    def chunk(self, s, h, slot):
        return self.win(s, h).at[self.at(slot)]

    def _send(self, cond, s, h, k, src, dst, recv, device):
        def copy():
            return pltpu.make_async_remote_copy(
                src_ref=src, dst_ref=dst, send_sem=self.send_sem.at[s, h, k], recv_sem=recv,
                device_id=device, device_id_type=MESH,
            )

        def go():
            copy().wait_send() if self.draining else copy().start()

        go() if cond is None else pl.when(cond)(go)

    def between(self, s):
        return (self.p.g < LAST, 2) if s == 0 else (self.p.g > 0, -2)

    def put(self, cond, s, h, k, slot, device, to_s, to):
        dst = self.win(to_s, h).at[self.at(to)]
        self._send(cond, s, h, k, self.chunk(s, h, slot), dst, self.recv_sem.at[to_s, h, to], device)

    def onward(self, s, h, slot, cond=None):
        p = self.p
        goes, step = self.between(s)
        goes = goes if cond is None else jnp.logical_and(goes, cond)
        self.put(goes, s, h, 6 - slot, slot, (p.w + step, p.n), s, slot - 4)

    def spread(self, s, h, slot, cond):
        p = self.p
        self.put(cond, s, h, 3, slot, (p.across, p.c), s, 4 + p.yhi)
        self.put(cond, s, h, 4, slot, (p.across, 2 + p.c), s, 3 + p.yhi)

    def fold(self, h):
        p = self.p
        both = jnp.logical_and
        near = both(p.g == LAST - 1, p.ylo == 1)
        here = p.g == LAST
        self.put(near, 0, h, 7, OWN, (p.w + 2, p.n), 1, 0)
        self.put(both(near, p.yhi == 1), 0, h, 8, OWN, (p.w + 2, p.c), 1, 1)
        self.put(here, 0, h, 0, OWN, (p.across, p.n), 1, 2)
        self.put(both(here, p.yhi == 0), 0, h, 1, OWN, (p.across, p.n + 2), 1, 1)
        self.put(both(both(here, p.ylo == 0), p.yhi == 1), 0, h, 1, OWN, (p.w, p.n - 2), 1, 1)
        self.inside(both(here, p.ylo == 0), h, 1, 0)
        for slot in range(3):
            self.inside(p.g == 0, h, 0, slot)

    def share(self, s, h, slot, cond=None):
        if self.draining:
            return
        p = self.p
        if slot == 0:
            cond = p.c == 1 if cond is None else jnp.logical_and(cond, p.c == 1)
        if slot == OWN:
            cond = p.c == 0 if cond is None else jnp.logical_and(cond, p.c == 0)
        at = slot - 1 + p.c
        src, dst = self.chunk(s, h, slot), self.win(s, h).at[2 * at + 1]

        def go():
            pltpu.make_async_remote_copy(
                src_ref=src, dst_ref=dst, send_sem=self.sib_sem.at[0, s, h], recv_sem=self.sib_sem.at[1, s, h],
                device_id=(p.w, p.sibling), device_id_type=MESH,
            ).start()

        go() if cond is None else pl.when(cond)(go)

    def inside(self, cond, h, s, slot):
        if self.draining:
            return
        pl.when(cond)(
            lambda: pltpu.make_async_copy(
                self.chunk(0, h, OWN), self.chunk(s, h, slot), self.recv_sem.at[s, h, slot]
            ).start()
        )

    def await_slot(self, s, h, slot, cond=None):
        if self.draining:
            return
        if cond is not None:
            pl.when(cond)(lambda: self.await_slot(s, h, slot))
            return
        ref = self.chunk(s, h, slot)
        pltpu.make_async_copy(ref, ref, self.recv_sem.at[s, h, slot]).wait()

    def roles(self, s):
        p = self.p
        first = p.ylo == s
        second = p.ylo != s
        low, high = p.yhi == 0, p.yhi == 1
        both = jnp.logical_and
        return first, second, both(first, low), both(first, high), both(second, low), both(second, high)

    def over(self, s, h, k, slot, half, to, cond):
        self.put(cond, s, h, k, slot, (self.p.across, 2 * half + self.p.c), s, to)

    def phase(self, number, s, h):
        p = self.p
        F, S, Fl, Fh, Sl, Sh = self.roles(s)
        low, high = p.yhi == 0, p.yhi == 1
        parity = h % 2
        carrier = jnp.logical_and(F, p.yhi == parity)

        def take(slot, cond=None, on=False):
            self.await_slot(s, h, slot, cond)
            if on:
                self.onward(s, h, slot, cond)

        if number == 0:
            self.onward(s, h, OWN)
            self.spread(s, h, OWN, F)
            self.over(s, h, 5, OWN, parity, FLOW, Sl)
            self.share(s, h, OWN)
            if s == 0:
                self.fold(h)
        elif number == 1:
            take(2)
            self.spread(s, h, 2, S)
            self.share(s, h, 2)
            take(5, Sl, True)
            self.share(s, h, 5, Sl)
            take(4, S, True)
            self.share(s, h, 4, S)
            take(3, Sh)
            self.over(s, h, 5, 3, 1, 5, Sh)
            self.share(s, h, 3, Sh)
            take(FLOW, carrier)
            self.over(s, h, 6, FLOW, 1, 5, carrier)
        elif number == 2:
            take(0, S)
            self.over(s, h, 6, 0, 0, 3, Sh)
            self.share(s, h, 0, S)
            take(1, Sl)
            self.share(s, h, 1, Sl)
            take(5, Fl)
            self.over(s, h, 5, 5, 0, 3, Fl)
            self.onward(s, h, 5, Fl)
            self.share(s, h, 5, Fl)
            take(4, F, True)
            self.share(s, h, 4, F)
            take(3, Fh)
            self.share(s, h, 3, Fh)
            take(5, high, True)
            self.share(s, h, 5, high)
        elif number == 3:
            take(3, low)
            self.share(s, h, 3, low)
            take(0, F)
            self.share(s, h, 0, F)
            rest = jnp.logical_not(Sl)
            take(1, rest)
            self.share(s, h, 1, rest)

    def arrived(self, s, h):
        ref = self.win(s, h).at[0:6]
        for way in (1, 0):
            pltpu.make_async_copy(ref, ref, self.sib_sem.at[way, s, h]).wait()


def greet(p):
    barrier = pltpu.get_barrier_semaphore()

    def signal(device):
        pl.semaphore_signal(barrier, inc=1, device_id=device, device_id_type=MESH)

    def pair(wide):
        signal((wide, p.c))
        signal((wide, 2 + p.c))

    both = jnp.logical_and
    top = p.g // LAST
    below = p.g // (LAST - 1) - top
    up, down = 1 - top, 1 - (LAST - p.g) // LAST
    pair(p.across)
    signal((p.w, p.sibling))
    pl.when(p.g < LAST)(lambda: signal((p.w + 2, p.n)))
    pl.when(p.g > 0)(lambda: signal((p.w - 2, p.n)))
    pl.when(both(p.g == LAST, p.ylo == 0))(lambda: signal((p.w, p.n + 2 - 4 * p.yhi)))
    pl.when(both(both(p.g == LAST - 1, p.ylo == 1), p.yhi == 1))(lambda: signal((p.w + 2, p.c)))
    pl.when(both(both(p.g == LAST, p.ylo == 1), p.yhi == 0))(lambda: signal((p.w - 2, 2 + p.c)))
    turn = p.ylo * (below * p.yhi + top * (1 - p.yhi)) + top * (1 - p.ylo)
    pl.semaphore_wait(barrier, 3 + up + down + turn)


def masks(start, lengths_ref, key_side, query_side, reach):
    lane = lax.broadcasted_iota(jnp.int32, (1, 128), 1)
    begins = jnp.zeros((1, 128), jnp.int32)
    ends = jnp.zeros((1, 128), jnp.int32)
    for e in range(NDOCS):
        length = lengths_ref[e]
        begins = begins + jnp.where(lane > e, length, 0)
        ends = ends + jnp.where(lane >= e, length, 0)
    back = jnp.where(begins <= start, begins, 0) - (start - (KEYS - ROWS))
    reach[...] = jnp.broadcast_to(back, (8, 128)).astype(jnp.float32)
    lanes = lax.broadcasted_iota(jnp.int32, (KEYS, 128), 1)
    place = lax.broadcasted_iota(jnp.int32, (KEYS, 128), 0) - (KEYS - ROWS)
    pos = place + start
    in_doc = ((pos >= begins) & (pos < ends)) | (pos < 0)
    own = place == lanes - NDOCS
    key_side[...] = jnp.where(((lanes < NDOCS) & in_doc) | ((lanes >= NDOCS) & own), 1.0, 0.0).astype(jnp.bfloat16)
    lanes = lax.broadcasted_iota(jnp.int32, (ROWS, 128), 1)
    row = lax.broadcasted_iota(jnp.int32, (ROWS, 128), 0)
    pos = row + start
    other = (pos < begins) | (pos >= ends)
    later = lanes - NDOCS > row
    query_side[...] = jnp.where(((lanes < NDOCS) & other) | (later & (lanes >= NDOCS)), MASKED, 0.0).astype(jnp.bfloat16)


TILE_HEADS = 4
PARTS = ((0, 256), (256, 512), (512, 768), (768, 896))


def attend(q_ref, side_ref, keys_side_ref, win_ref, h, row, write, base=0):
    rate = math.log2(math.e) / math.sqrt(HEAD_DIM)
    k = win_ref[:, :, 0:HEAD_DIM].reshape(KEYS, HEAD_DIM)
    v = win_ref[:, :, HEAD_DIM : 2 * HEAD_DIM].reshape(KEYS, HEAD_DIM)
    k = jnp.concatenate([k, keys_side_ref[...]], axis=1)
    v = jnp.concatenate([v, jnp.ones((KEYS, HEAD_DIM), jnp.bfloat16)], axis=1)
    if base:
        k, v = k[base:], v[base:]
        parts = [(at, at + 256) for at in range(0, KEYS - base, 256)]
    else:
        k = jnp.concatenate([k, k[KEYS - ROWS :]], axis=0)
        v = jnp.concatenate([v, jnp.zeros((ROWS, 2 * HEAD_DIM), jnp.bfloat16)], axis=0)
        parts = PARTS
    side = side_ref[...]
    tiles = SHARE // TILE_HEADS

    def columns(a):
        return pl.ds(pl.multiple_of((h * SHARE + a) * HEAD_DIM, HEAD_DIM), HEAD_DIM)

    def queries(t):
        heads = range(t * TILE_HEADS, (t + 1) * TILE_HEADS)
        return jnp.concatenate(
            [jnp.concatenate([q_ref[row : row + ROWS, columns(a)], side], axis=1) for a in heads], axis=0
        )

    def score(q, part):
        low, high = part
        return lax.dot_general(q, k[low:high], (((1,), (1,)), ((), ())), preferred_element_type=jnp.float32)

    q = queries(0)
    ahead = [score(q, part) for part in parts]
    for t in range(tiles):
        scores, ahead = ahead, []
        if t + 1 < tiles:
            q = queries(t + 1)
        top = functools.reduce(
            jnp.maximum, [s[:, at : at + 128] for s in scores for at in range(0, s.shape[1], 128)]
        )
        top = jnp.max(top, axis=1, keepdims=True)
        mixed = None
        for part, s in zip(parts, scores):
            if t + 1 < tiles:
                ahead.append(score(q, part))
            weights = jnp.exp2((s - top) * rate).astype(jnp.bfloat16)
            new = jnp.dot(weights, v[part[0] : part[1]], preferred_element_type=jnp.float32)
            mixed = new if mixed is None else mixed + new
        mixed = mixed[:, 0:HEAD_DIM] / mixed[:, HEAD_DIM : 2 * HEAD_DIM]
        for i in range(TILE_HEADS):
            write(t * TILE_HEADS + i, mixed[i * ROWS : (i + 1) * ROWS])


def kernel(
    order_hbm, lengths_hbm, q_hbm, k_hbm, v_hbm, out_ref, win, q_ref, key_side, query_side, reach, order_ref, lengths_ref,
    k_ref, v_ref, in_sem, send_sem, recv_sem, sib_sem,
):
    p = Place()
    loads = [
        pltpu.make_async_copy(src, dst, in_sem.at[i])
        for i, (src, dst) in enumerate(
            ((order_hbm, order_ref), (k_hbm, k_ref), (v_hbm, v_ref), (lengths_hbm, lengths_ref), (q_hbm, q_ref))
        )
    ]
    for load in loads:
        load.start()
    greet(p)
    for load in loads[:4]:
        load.wait()
    first = order_ref[0, p.w]
    reach[2] = jnp.full((8, 128), first, jnp.int32).astype(jnp.float32)

    def swapped(width):
        return jnp.full((ROWS, width), first, jnp.int32) >= 64

    def own(h):
        cols = pl.ds(pl.multiple_of(h * HEAD_DIM, HEAD_DIM), HEAD_DIM)
        other = swapped(HEAD_DIM)
        for part, ref in enumerate((k_ref, v_ref)):
            low, high = ref[0:ROWS, cols], ref[ROWS : 2 * ROWS, cols]
            to = slice(part * HEAD_DIM, (part + 1) * HEAD_DIM)
            win[0, h, 12, :, to] = jnp.where(other, high, low)
            win[1, h, 12, :, to] = jnp.where(other, low, high)
        for s in range(2):
            ex.phase(0, s, h)

    ex = Exchange(p, lambda s, h: win.at[s, h], send_sem, recv_sem, sib_sem)

    def turn_queries(i, carry):
        wide = 1024
        cols = pl.ds(pl.multiple_of(i * wide, wide), wide)
        low, high = q_ref[0:ROWS, cols], q_ref[ROWS : 2 * ROWS, cols]
        other = swapped(wide)
        q_ref[0:ROWS, cols] = jnp.where(other, high, low)
        q_ref[ROWS : 2 * ROWS, cols] = jnp.where(other, low, high)
        return carry

    def unit(s, h):
        def write(a, mixed):
            cols = pl.ds(pl.multiple_of((h * SHARE + a) * HEAD_DIM, HEAD_DIM), HEAD_DIM)
            out_ref[s, :, cols] = mixed

        ex.arrived(s, h)
        attend(q_ref, query_side.at[s], key_side.at[s], win.at[s, h, 0:CHUNKS], h, s * ROWS, write)

    def both(number, h):
        for s in range(2):
            ex.phase(number, s, h)

    def fill(t, carry):
        own(t)

        @pl.when(t == 0)
        def _():
            masks(p.w * GROUP + p.n * ROWS, lengths_ref, key_side.at[0], query_side.at[0], reach.at[0])
            masks((2 * 64 - 1 - p.w) * GROUP + p.n * ROWS, lengths_ref, key_side.at[1], query_side.at[1], reach.at[1])

        @pl.when(t == 1)
        def _():
            loads[4].wait()
            lax.fori_loop(0, 8, turn_queries, 0)

        for number in range(1, 4):
            pl.when(t >= number)(lambda number=number: both(number, t - number))
        return carry

    def work(h, carry):
        pl.when(h + 3 < KV_HEADS)(lambda: both(1, h + 3))
        unit(1, h)
        for number, later in ((2, 2), (3, 1)):
            pl.when(h + later < KV_HEADS)(lambda number=number, later=later: both(number, h + later))
        unit(0, h)
        return carry

    lax.fori_loop(0, KV_HEADS, fill, 0)
    lax.fori_loop(0, KV_HEADS - 1, work, 0)
    for s in range(2):
        ex.arrived(s, KV_HEADS - 1)
    ex.draining = True

    def drain(h, carry):
        for number in range(3):
            both(number, h)
        return carry

    lax.fori_loop(0, KV_HEADS, drain, 0)


def last_kernel(part_ref, win, q_ref, key_side, query_side, reach, out_hbm, o_ref, part_sem, out_sem):
    width = SHARE * HEAD_DIM
    flip = (jnp.max(reach[2]) >= 64).astype(jnp.int32)
    rows = [pl.ds(pl.multiple_of(at * ROWS, ROWS), ROWS) for at in (flip, 1 - flip)]
    firsts = [
        pltpu.make_async_copy(part_ref.at[s], out_hbm.at[rows[s], 0 : FIRST_HEADS * width], part_sem.at[s])
        for s in range(2)
    ]
    for copy in firsts:
        copy.start()
    backs = [jnp.max(reach[s]) for s in range(2)]

    tiles, wide = SHARE // TILE_HEADS, TILE_HEADS * HEAD_DIM

    def put(s, tile):
        cols = slice(tile * wide, (tile + 1) * wide)
        to = pl.ds(FIRST_HEADS * width + tile * wide, wide)
        return pltpu.make_async_copy(o_ref.at[s, :, cols], out_hbm.at[rows[s], to], out_sem.at[s, tile])

    for s in (1, 0):

        def write(a, mixed, s=s):
            o_ref[s, :, a * HEAD_DIM : (a + 1) * HEAD_DIM] = mixed
            if a % TILE_HEADS == TILE_HEADS - 1:
                put(s, a // TILE_HEADS).start()

        def take(base, s=s, write=write):
            attend(
                q_ref, query_side.at[s], key_side.at[s], win.at[s, FIRST_HEADS, 0:CHUNKS], FIRST_HEADS, s * ROWS, write, base
            )

        back = backs[s]
        pl.when(back >= 320)(lambda take=take: take(320))
        pl.when(jnp.logical_and(back >= 64, back < 320))(lambda take=take: take(64))
        pl.when(back < 64)(lambda take=take: take(0))
    for copy in firsts:
        copy.wait()
    for s in range(2):
        for tile in range(tiles):
            put(s, tile).wait()


def attention(block_order, doc_lengths, queries, keys, values):
    held = pl.BlockSpec(memory_space=pltpu.HBM)
    near = pl.BlockSpec(memory_space=pltpu.VMEM)
    width = SHARE * HEAD_DIM
    flops = 2 * ROWS * SHARE * KEYS * 512
    operands = [
        pltpu.with_memory_space_constraint(a, pltpu.HBM) for a in (block_order, doc_lengths, queries, keys, values)
    ]
    parts = pl.pallas_call(
        kernel,
        out_shape=(
            pltpu.VMEM((2, ROWS, FIRST_HEADS * width), jnp.float32),
            pltpu.VMEM((2, KV_HEADS, CHUNKS + 1, ROWS, 2 * HEAD_DIM), jnp.bfloat16),
            pltpu.VMEM(queries.shape, jnp.bfloat16),
            pltpu.VMEM((2, KEYS, HEAD_DIM), jnp.bfloat16),
            pltpu.VMEM((2, ROWS, HEAD_DIM), jnp.bfloat16),
            pltpu.VMEM((3, 8, 128), jnp.float32),
        ),
        in_specs=[held] * 5,
        out_specs=(near,) * 6,
        scratch_shapes=[
            pltpu.SMEM((2, 64), jnp.int32),
            pltpu.SMEM((NDOCS,), jnp.int32),
            pltpu.VMEM((2 * ROWS, KV_HEADS * HEAD_DIM), jnp.bfloat16),
            pltpu.VMEM((2 * ROWS, KV_HEADS * HEAD_DIM), jnp.bfloat16),
            pltpu.SemaphoreType.DMA((5,)),
            pltpu.SemaphoreType.DMA((2, KV_HEADS, 9)),
            pltpu.SemaphoreType.DMA((2, KV_HEADS, 8)),
            pltpu.SemaphoreType.DMA((2, 2, KV_HEADS)),
        ],
        compiler_params=pltpu.CompilerParams(collective_id=0, has_side_effects=True, vmem_limit_bytes=32 << 20),
        cost_estimate=pl.CostEstimate(flops=2 * FIRST_HEADS * flops, bytes_accessed=4 << 20, transcendentals=0),
        name="exchange_attend",
    )(*operands)
    return pl.pallas_call(
        last_kernel,
        out_shape=jax.ShapeDtypeStruct(queries.shape, jnp.float32),
        in_specs=[near] * 6,
        out_specs=held,
        scratch_shapes=[
            pltpu.VMEM((2, ROWS, width), jnp.float32),
            pltpu.SemaphoreType.DMA((2,)),
            pltpu.SemaphoreType.DMA((2, SHARE // TILE_HEADS)),
        ],
        compiler_params=pltpu.CompilerParams(vmem_limit_bytes=32 << 20),
        cost_estimate=pl.CostEstimate(flops=2 * (KV_HEADS - FIRST_HEADS) * flops, bytes_accessed=4 << 20, transcendentals=0),
        name="attend_last",
    )(*parts)


def body(queries, keys, values, block_order, doc_lengths):
    return attention(block_order.T, doc_lengths, queries, keys, values)


def solution(mesh):
    rows = P(("wide", "narrow"), None)
    return jax.shard_map(
        body, mesh=mesh, in_specs=(rows, rows, rows, P(), P()), out_specs=rows, check_vma=False
    )
```

```python
import functools
import math

import jax
import jax.numpy as jnp
from jax import lax
from jax.experimental import pallas as pl
from jax.experimental.pallas import tpu as pltpu
from jax.sharding import PartitionSpec as P

MESH = pl.DeviceIdType.MESH
QUERY_HEADS = 64
KV_HEADS = 4
HEAD_DIM = 128
SHARE = QUERY_HEADS // KV_HEADS
GROUP = 256
ROWS = 64
CHUNKS = 13
KEYS = CHUNKS * ROWS
NDOCS = 64
FIRST_HEADS = KV_HEADS - 1
OWN = 6
FLOW = 7
LAST = 31
MASKED = -1e30


class Place:
    def __init__(self):
        self.w = lax.axis_index("wide")
        self.n = lax.axis_index("narrow")
        self.g = self.w // 2
        self.ylo = self.w % 2
        self.yhi = self.n // 2
        self.c = self.n % 2
        self.across = self.w + 1 - 2 * self.ylo
        self.sibling = self.n + 1 - 2 * self.c


class Exchange:
    def __init__(self, place, win, send_sem, recv_sem, sib_sem):
        self.p = place
        self.win, self.send_sem, self.recv_sem, self.sib_sem = win, send_sem, recv_sem, sib_sem
        self.draining = False

    @staticmethod
    def at(slot):
        return 13 if isinstance(slot, int) and slot == FLOW else 2 * slot

    def chunk(self, s, h, slot):
        return self.win(s, h).at[self.at(slot)]

    def _send(self, cond, s, h, k, src, dst, recv, device):
        def copy():
            return pltpu.make_async_remote_copy(
                src_ref=src, dst_ref=dst, send_sem=self.send_sem.at[s, h, k], recv_sem=recv,
                device_id=device, device_id_type=MESH,
            )

        def go():
            copy().wait_send() if self.draining else copy().start()

        go() if cond is None else pl.when(cond)(go)

    def between(self, s):
        return (self.p.g < LAST, 2) if s == 0 else (self.p.g > 0, -2)

    def put(self, cond, s, h, k, slot, device, to_s, to):
        dst = self.win(to_s, h).at[self.at(to)]
        self._send(cond, s, h, k, self.chunk(s, h, slot), dst, self.recv_sem.at[to_s, h, to], device)

    def onward(self, s, h, slot, cond=None):
        p = self.p
        goes, step = self.between(s)
        goes = goes if cond is None else jnp.logical_and(goes, cond)
        self.put(goes, s, h, 6 - slot, slot, (p.w + step, p.n), s, slot - 4)

    def spread(self, s, h, slot, cond):
        p = self.p
        self.put(cond, s, h, 3, slot, (p.across, p.c), s, 4 + p.yhi)
        self.put(cond, s, h, 4, slot, (p.across, 2 + p.c), s, 3 + p.yhi)

    def fold(self, h):
        p = self.p
        both = jnp.logical_and
        near = both(p.g == LAST - 1, p.ylo == 1)
        here = p.g == LAST
        self.put(near, 0, h, 7, OWN, (p.w + 2, p.n), 1, 0)
        self.put(both(near, p.yhi == 1), 0, h, 8, OWN, (p.w + 2, p.c), 1, 1)
        self.put(here, 0, h, 0, OWN, (p.across, p.n), 1, 2)
        self.put(both(here, p.yhi == 0), 0, h, 1, OWN, (p.across, p.n + 2), 1, 1)
        self.put(both(both(here, p.ylo == 0), p.yhi == 1), 0, h, 1, OWN, (p.w, p.n - 2), 1, 1)
        self.inside(both(here, p.ylo == 0), h, 1, 0)
        for slot in range(3):
            self.inside(p.g == 0, h, 0, slot)

    def share(self, s, h, slot, cond=None):
        if self.draining:
            return
        p = self.p
        if slot == 0:
            cond = p.c == 1 if cond is None else jnp.logical_and(cond, p.c == 1)
        if slot == OWN:
            cond = p.c == 0 if cond is None else jnp.logical_and(cond, p.c == 0)
        at = slot - 1 + p.c
        src, dst = self.chunk(s, h, slot), self.win(s, h).at[2 * at + 1]

        def go():
            pltpu.make_async_remote_copy(
                src_ref=src, dst_ref=dst, send_sem=self.sib_sem.at[0, s, h], recv_sem=self.sib_sem.at[1, s, h],
                device_id=(p.w, p.sibling), device_id_type=MESH,
            ).start()

        go() if cond is None else pl.when(cond)(go)

    def inside(self, cond, h, s, slot):
        if self.draining:
            return
        pl.when(cond)(
            lambda: pltpu.make_async_copy(
                self.chunk(0, h, OWN), self.chunk(s, h, slot), self.recv_sem.at[s, h, slot]
            ).start()
        )

    def await_slot(self, s, h, slot, cond=None):
        if self.draining:
            return
        if cond is not None:
            pl.when(cond)(lambda: self.await_slot(s, h, slot))
            return
        ref = self.chunk(s, h, slot)
        pltpu.make_async_copy(ref, ref, self.recv_sem.at[s, h, slot]).wait()

    def roles(self, s):
        p = self.p
        first = p.ylo == s
        second = p.ylo != s
        low, high = p.yhi == 0, p.yhi == 1
        both = jnp.logical_and
        return first, second, both(first, low), both(first, high), both(second, low), both(second, high)

    def over(self, s, h, k, slot, half, to, cond):
        self.put(cond, s, h, k, slot, (self.p.across, 2 * half + self.p.c), s, to)

    def phase(self, number, s, h):
        p = self.p
        F, S, Fl, Fh, Sl, Sh = self.roles(s)
        low, high = p.yhi == 0, p.yhi == 1
        parity = h % 2
        carrier = jnp.logical_and(F, p.yhi == parity)

        def take(slot, cond=None, on=False):
            self.await_slot(s, h, slot, cond)
            if on:
                self.onward(s, h, slot, cond)

        if number == 0:
            self.onward(s, h, OWN)
            self.spread(s, h, OWN, F)
            self.over(s, h, 5, OWN, parity, FLOW, Sl)
            self.share(s, h, OWN)
            if s == 0:
                self.fold(h)
        elif number == 1:
            take(2)
            self.spread(s, h, 2, S)
            self.share(s, h, 2)
            take(5, Sl, True)
            self.share(s, h, 5, Sl)
            take(4, S, True)
            self.share(s, h, 4, S)
            take(3, Sh)
            self.over(s, h, 5, 3, 1, 5, Sh)
            self.share(s, h, 3, Sh)
            take(FLOW, carrier)
            self.over(s, h, 6, FLOW, 1, 5, carrier)
        elif number == 2:
            take(0, S)
            self.over(s, h, 6, 0, 0, 3, Sh)
            self.share(s, h, 0, S)
            take(1, Sl)
            self.share(s, h, 1, Sl)
            take(5, Fl)
            self.over(s, h, 5, 5, 0, 3, Fl)
            self.onward(s, h, 5, Fl)
            self.share(s, h, 5, Fl)
            take(4, F, True)
            self.share(s, h, 4, F)
            take(3, Fh)
            self.share(s, h, 3, Fh)
            take(5, high, True)
            self.share(s, h, 5, high)
        elif number == 3:
            take(3, low)
            self.share(s, h, 3, low)
            take(0, F)
            self.share(s, h, 0, F)
            rest = jnp.logical_not(Sl)
            take(1, rest)
            self.share(s, h, 1, rest)

    def arrived(self, s, h):
        ref = self.win(s, h).at[0:6]
        for way in (1, 0):
            pltpu.make_async_copy(ref, ref, self.sib_sem.at[way, s, h]).wait()


def greet(p):
    barrier = pltpu.get_barrier_semaphore()

    def signal(device):
        pl.semaphore_signal(barrier, inc=1, device_id=device, device_id_type=MESH)

    def pair(wide):
        signal((wide, p.c))
        signal((wide, 2 + p.c))

    both = jnp.logical_and
    top = p.g // LAST
    below = p.g // (LAST - 1) - top
    up, down = 1 - top, 1 - (LAST - p.g) // LAST
    pair(p.across)
    signal((p.w, p.sibling))
    pl.when(p.g < LAST)(lambda: signal((p.w + 2, p.n)))
    pl.when(p.g > 0)(lambda: signal((p.w - 2, p.n)))
    pl.when(both(p.g == LAST, p.ylo == 0))(lambda: signal((p.w, p.n + 2 - 4 * p.yhi)))
    pl.when(both(both(p.g == LAST - 1, p.ylo == 1), p.yhi == 1))(lambda: signal((p.w + 2, p.c)))
    pl.when(both(both(p.g == LAST, p.ylo == 1), p.yhi == 0))(lambda: signal((p.w - 2, 2 + p.c)))
    turn = p.ylo * (below * p.yhi + top * (1 - p.yhi)) + top * (1 - p.ylo)
    pl.semaphore_wait(barrier, 3 + up + down + turn)


def masks(start, lengths_ref, key_side, query_side, reach):
    lane = lax.broadcasted_iota(jnp.int32, (1, 128), 1)
    begins = jnp.zeros((1, 128), jnp.int32)
    ends = jnp.zeros((1, 128), jnp.int32)
    for e in range(NDOCS):
        length = lengths_ref[e]
        begins = begins + jnp.where(lane > e, length, 0)
        ends = ends + jnp.where(lane >= e, length, 0)
    back = jnp.where(begins <= start, begins, 0) - (start - (KEYS - ROWS))
    reach[...] = jnp.broadcast_to(back, (8, 128)).astype(jnp.float32)
    lanes = lax.broadcasted_iota(jnp.int32, (KEYS, 128), 1)
    place = lax.broadcasted_iota(jnp.int32, (KEYS, 128), 0) - (KEYS - ROWS)
    pos = place + start
    in_doc = ((pos >= begins) & (pos < ends)) | (pos < 0)
    own = place == lanes - NDOCS
    key_side[...] = jnp.where(((lanes < NDOCS) & in_doc) | ((lanes >= NDOCS) & own), 1.0, 0.0).astype(jnp.bfloat16)
    lanes = lax.broadcasted_iota(jnp.int32, (ROWS, 128), 1)
    row = lax.broadcasted_iota(jnp.int32, (ROWS, 128), 0)
    pos = row + start
    other = (pos < begins) | (pos >= ends)
    later = lanes - NDOCS > row
    query_side[...] = jnp.where(((lanes < NDOCS) & other) | (later & (lanes >= NDOCS)), MASKED, 0.0).astype(jnp.bfloat16)


TILE_HEADS = 4
PARTS = ((0, 256), (256, 512), (512, 768), (768, 896))


def attend(q_ref, side_ref, keys_side_ref, win_ref, h, row, write, base=0):
    rate = math.log2(math.e) / math.sqrt(HEAD_DIM)
    k = win_ref[:, :, 0:HEAD_DIM].reshape(KEYS, HEAD_DIM)
    v = win_ref[:, :, HEAD_DIM : 2 * HEAD_DIM].reshape(KEYS, HEAD_DIM)
    k = jnp.concatenate([k, keys_side_ref[...]], axis=1)
    v = jnp.concatenate([v, jnp.ones((KEYS, HEAD_DIM), jnp.bfloat16)], axis=1)
    if base:
        k, v = k[base:], v[base:]
        parts = [(at, at + 256) for at in range(0, KEYS - base, 256)]
    else:
        k = jnp.concatenate([k, k[KEYS - ROWS :]], axis=0)
        v = jnp.concatenate([v, jnp.zeros((ROWS, 2 * HEAD_DIM), jnp.bfloat16)], axis=0)
        parts = PARTS
    side = side_ref[...]
    tiles = SHARE // TILE_HEADS

    def columns(a):
        return pl.ds(pl.multiple_of((h * SHARE + a) * HEAD_DIM, HEAD_DIM), HEAD_DIM)

    def queries(t):
        heads = range(t * TILE_HEADS, (t + 1) * TILE_HEADS)
        return jnp.concatenate(
            [jnp.concatenate([q_ref[row : row + ROWS, columns(a)], side], axis=1) for a in heads], axis=0
        )

    def score(q, part):
        low, high = part
        return lax.dot_general(q, k[low:high], (((1,), (1,)), ((), ())), preferred_element_type=jnp.float32)

    q = queries(0)
    ahead = [score(q, part) for part in parts]
    for t in range(tiles):
        scores, ahead = ahead, []
        if t + 1 < tiles:
            q = queries(t + 1)
        top = functools.reduce(
            jnp.maximum, [s[:, at : at + 128] for s in scores for at in range(0, s.shape[1], 128)]
        )
        top = jnp.max(top, axis=1, keepdims=True)
        mixed = None
        for part, s in zip(parts, scores):
            if t + 1 < tiles:
                ahead.append(score(q, part))
            weights = jnp.exp2((s - top) * rate).astype(jnp.bfloat16)
            new = jnp.dot(weights, v[part[0] : part[1]], preferred_element_type=jnp.float32)
            mixed = new if mixed is None else mixed + new
        mixed = mixed[:, 0:HEAD_DIM] / mixed[:, HEAD_DIM : 2 * HEAD_DIM]
        for i in range(TILE_HEADS):
            write(t * TILE_HEADS + i, mixed[i * ROWS : (i + 1) * ROWS])


def kernel(
    order_hbm, lengths_hbm, q_hbm, k_hbm, v_hbm, out_ref, win, q_ref, key_side, query_side, reach, order_ref, lengths_ref,
    k_ref, v_ref, in_sem, send_sem, recv_sem, sib_sem,
):
    p = Place()
    loads = [
        pltpu.make_async_copy(src, dst, in_sem.at[i])
        for i, (src, dst) in enumerate(
            ((order_hbm, order_ref), (k_hbm, k_ref), (v_hbm, v_ref), (lengths_hbm, lengths_ref), (q_hbm, q_ref))
        )
    ]
    for load in loads:
        load.start()
    greet(p)
    for load in loads[:4]:
        load.wait()
    first = order_ref[0, p.w]
    reach[2] = jnp.full((8, 128), first, jnp.int32).astype(jnp.float32)

    def swapped(width):
        return jnp.full((ROWS, width), first, jnp.int32) >= 64

    def own(h):
        cols = pl.ds(pl.multiple_of(h * HEAD_DIM, HEAD_DIM), HEAD_DIM)
        other = swapped(HEAD_DIM)
        for part, ref in enumerate((k_ref, v_ref)):
            low, high = ref[0:ROWS, cols], ref[ROWS : 2 * ROWS, cols]
            to = slice(part * HEAD_DIM, (part + 1) * HEAD_DIM)
            win[0, h, 12, :, to] = jnp.where(other, high, low)
            win[1, h, 12, :, to] = jnp.where(other, low, high)
        for s in range(2):
            ex.phase(0, s, h)

    ex = Exchange(p, lambda s, h: win.at[s, h], send_sem, recv_sem, sib_sem)

    def turn_queries(i, carry):
        wide = 1024
        cols = pl.ds(pl.multiple_of(i * wide, wide), wide)
        low, high = q_ref[0:ROWS, cols], q_ref[ROWS : 2 * ROWS, cols]
        other = swapped(wide)
        q_ref[0:ROWS, cols] = jnp.where(other, high, low)
        q_ref[ROWS : 2 * ROWS, cols] = jnp.where(other, low, high)
        return carry

    def unit(s, h):
        def write(a, mixed):
            cols = pl.ds(pl.multiple_of((h * SHARE + a) * HEAD_DIM, HEAD_DIM), HEAD_DIM)
            out_ref[s, :, cols] = mixed

        ex.arrived(s, h)
        attend(q_ref, query_side.at[s], key_side.at[s], win.at[s, h, 0:CHUNKS], h, s * ROWS, write)

    def both(number, h):
        for s in (1, 0):
            ex.phase(number, s, h)

    def fill(t, carry):
        own(t)

        @pl.when(t == 0)
        def _():
            masks(p.w * GROUP + p.n * ROWS, lengths_ref, key_side.at[0], query_side.at[0], reach.at[0])
            masks((2 * 64 - 1 - p.w) * GROUP + p.n * ROWS, lengths_ref, key_side.at[1], query_side.at[1], reach.at[1])

        @pl.when(t == 1)
        def _():
            loads[4].wait()
            lax.fori_loop(0, 8, turn_queries, 0)

        for number in range(1, 4):
            pl.when(t >= number)(lambda number=number: both(number, t - number))
        return carry

    def work(h, carry):
        pl.when(h + 3 < KV_HEADS)(lambda: both(1, h + 3))
        unit(1, h)
        for number, later in ((2, 2), (3, 1)):
            pl.when(h + later < KV_HEADS)(lambda number=number, later=later: both(number, h + later))
        unit(0, h)
        return carry

    lax.fori_loop(0, KV_HEADS, fill, 0)
    lax.fori_loop(0, KV_HEADS - 1, work, 0)
    for s in range(2):
        ex.arrived(s, KV_HEADS - 1)
    ex.draining = True

    def drain(h, carry):
        for number in range(3):
            both(number, h)
        return carry

    lax.fori_loop(0, KV_HEADS, drain, 0)


def last_kernel(part_ref, win, q_ref, key_side, query_side, reach, out_hbm, o_ref, part_sem, out_sem):
    width = SHARE * HEAD_DIM
    flip = (jnp.max(reach[2]) >= 64).astype(jnp.int32)
    rows = [pl.ds(pl.multiple_of(at * ROWS, ROWS), ROWS) for at in (flip, 1 - flip)]
    firsts = [
        pltpu.make_async_copy(part_ref.at[s], out_hbm.at[rows[s], 0 : FIRST_HEADS * width], part_sem.at[s])
        for s in range(2)
    ]
    for copy in firsts:
        copy.start()
    backs = [jnp.max(reach[s]) for s in range(2)]

    tiles, wide = SHARE // TILE_HEADS, TILE_HEADS * HEAD_DIM

    def put(s, tile):
        cols = slice(tile * wide, (tile + 1) * wide)
        to = pl.ds(FIRST_HEADS * width + tile * wide, wide)
        return pltpu.make_async_copy(o_ref.at[s, :, cols], out_hbm.at[rows[s], to], out_sem.at[s, tile])

    for s in (1, 0):

        def write(a, mixed, s=s):
            o_ref[s, :, a * HEAD_DIM : (a + 1) * HEAD_DIM] = mixed
            if a % TILE_HEADS == TILE_HEADS - 1:
                put(s, a // TILE_HEADS).start()

        def take(base, s=s, write=write):
            attend(
                q_ref, query_side.at[s], key_side.at[s], win.at[s, FIRST_HEADS, 0:CHUNKS], FIRST_HEADS, s * ROWS, write, base
            )

        back = backs[s]
        pl.when(back >= 320)(lambda take=take: take(320))
        pl.when(jnp.logical_and(back >= 64, back < 320))(lambda take=take: take(64))
        pl.when(back < 64)(lambda take=take: take(0))
    for copy in firsts:
        copy.wait()
    for s in range(2):
        for tile in range(tiles):
            put(s, tile).wait()


def attention(block_order, doc_lengths, queries, keys, values):
    held = pl.BlockSpec(memory_space=pltpu.HBM)
    near = pl.BlockSpec(memory_space=pltpu.VMEM)
    width = SHARE * HEAD_DIM
    flops = 2 * ROWS * SHARE * KEYS * 512
    operands = [
        pltpu.with_memory_space_constraint(a, pltpu.HBM) for a in (block_order, doc_lengths, queries, keys, values)
    ]
    parts = pl.pallas_call(
        kernel,
        out_shape=(
            pltpu.VMEM((2, ROWS, FIRST_HEADS * width), jnp.float32),
            pltpu.VMEM((2, KV_HEADS, CHUNKS + 1, ROWS, 2 * HEAD_DIM), jnp.bfloat16),
            pltpu.VMEM(queries.shape, jnp.bfloat16),
            pltpu.VMEM((2, KEYS, HEAD_DIM), jnp.bfloat16),
            pltpu.VMEM((2, ROWS, HEAD_DIM), jnp.bfloat16),
            pltpu.VMEM((3, 8, 128), jnp.float32),
        ),
        in_specs=[held] * 5,
        out_specs=(near,) * 6,
        scratch_shapes=[
            pltpu.SMEM((2, 64), jnp.int32),
            pltpu.SMEM((NDOCS,), jnp.int32),
            pltpu.VMEM((2 * ROWS, KV_HEADS * HEAD_DIM), jnp.bfloat16),
            pltpu.VMEM((2 * ROWS, KV_HEADS * HEAD_DIM), jnp.bfloat16),
            pltpu.SemaphoreType.DMA((5,)),
            pltpu.SemaphoreType.DMA((2, KV_HEADS, 9)),
            pltpu.SemaphoreType.DMA((2, KV_HEADS, 8)),
            pltpu.SemaphoreType.DMA((2, 2, KV_HEADS)),
        ],
        compiler_params=pltpu.CompilerParams(collective_id=0, has_side_effects=True, vmem_limit_bytes=32 << 20),
        cost_estimate=pl.CostEstimate(flops=2 * FIRST_HEADS * flops, bytes_accessed=4 << 20, transcendentals=0),
        name="exchange_attend",
    )(*operands)
    return pl.pallas_call(
        last_kernel,
        out_shape=jax.ShapeDtypeStruct(queries.shape, jnp.float32),
        in_specs=[near] * 6,
        out_specs=held,
        scratch_shapes=[
            pltpu.VMEM((2, ROWS, width), jnp.float32),
            pltpu.SemaphoreType.DMA((2,)),
            pltpu.SemaphoreType.DMA((2, SHARE // TILE_HEADS)),
        ],
        compiler_params=pltpu.CompilerParams(vmem_limit_bytes=32 << 20),
        cost_estimate=pl.CostEstimate(flops=2 * (KV_HEADS - FIRST_HEADS) * flops, bytes_accessed=4 << 20, transcendentals=0),
        name="attend_last",
    )(*parts)


def body(queries, keys, values, block_order, doc_lengths):
    return attention(block_order.T, doc_lengths, queries, keys, values)


def solution(mesh):
    rows = P(("wide", "narrow"), None)
    return jax.shard_map(
        body, mesh=mesh, in_specs=(rows, rows, rows, P(), P()), out_specs=rows, check_vma=False
    )
```
